768 devices in a mesh: grp: 12 (over z), blk: 8 (over x, core), sub: 8 (over y).
Axes of the slice: x: 4, y: 8, z: 12, core: 2. Of those that a mesh axis runs over, the one named last changes fastest.
Arguments:
- mass_per_volume: float32 [32, 256, 1536], P('blk', 'sub', 'grp'), may hold values from 0.8 to 1.2
- flow_speed_vector: float32 [3, 32, 256, 1536], P(None, 'blk', 'sub', 'grp'), may hold values from -1 to 1
- normal_stress: float32 [32, 256, 1536], P('blk', 'sub', 'grp'), may hold values from 0.8 to 1.2
- facing_strip_index: int32 [12, 8, 256], P('grp', 'blk', 'sub'), may hold values from 0 to 511, as said below
- solid_kelvin: float32 [64, 64, 1536], P('blk', 'sub', 'grp'), may hold values from 0.5 to 1.5
- face_coupling: float32 [6, 64, 64, 1536], P(None, 'blk', 'sub', 'grp'), may hold values from 0 to 2, as said below
- substance_index: int32 [64, 64, 1536], P('blk', 'sub', 'grp'), may hold values from 0 to 7
- substance_storage: float32 [8], replicated, may hold values from 0.5 to 4
Outputs:
- fluid_next: float32 [5, 32, 256, 1536], P(None, 'blk', 'sub', 'grp')
- metal_next: float32 [64, 64, 1536], P('blk', 'sub', 'grp')
The draws below stay inside these ranges and needn't reach their ends.
Inputs may be any that keep to these rules, and one draw needn't show every extreme that they name: `facing_strip_index`: A value v names metal device v // 8 of the blade (devices numbered over blk then sub) and strip v % 8 on it. The strips of each fluid device name exactly 32 distinct metal devices, each exactly 1 times; strips within a metal device are named with any multiplicity. `face_coupling`: channels 0 to 2 are the conductances across the lower x, y and z face of each cell, channels 3 to 5 across the upper ones; a cell's upper conductance equals the lower one of the next cell along that dimension. Conductances across the grid's ends in x and y and across multiples of 128 along z are zero, all others lie in 0.2 to 2.
All inputs are finite; a program needn't handle non-finite values.
Results may differ from the reference program's by a relative error of at most 0.0001.
Values sent between devices are 32-bit elements; how exact they have to be, the bound alone decides.
A program may use at most 32 MiB of HBM per device.

```python
import math
import jax
import jax.numpy as jnp
from jax import lax

FX = 4
FY = 32
UNIT_SPAN_NODES = 128
UNIT_SOLID_ALONG = 8
UNIT_SOLID_ACROSS = 8
MATS = 8
ITERS = 4
NX = 32
NY = 256
SPAN_NODE_COUNT = 1536
SOLID_ALONG_NUM = 64
SOLID_ACROSS_NUM = 64
UNITS_PER_VANE = 64
CAP = 1


def draw_facing_strip_index(key, part):
    vane_sequence = SPAN_NODE_COUNT // UNIT_SPAN_NODES
    partition_sequence = NX // FX
    devices = vane_sequence * partition_sequence * (NY // FY)

    def one_device(device_key):
        key_first, key_second, key_third = jax.random.split(device_key, 3)
        chosen = jax.random.permutation(key_first, UNITS_PER_VANE)[:UNITS_PER_VANE // 2]
        targets = jnp.repeat(chosen, CAP, total_repeat_length=FY)
        targets = jax.random.permutation(key_second, targets)
        slot_ids = jax.random.randint(key_third, (FY,), 0, UNIT_SOLID_ACROSS)
        return (targets * UNIT_SOLID_ACROSS + slot_ids).astype(jnp.int32)
    rows = jax.vmap(one_device)(jax.random.split(key, devices))
    return rows.reshape(vane_sequence, partition_sequence, NY)


def draw_face_coupling(key, part):
    face_keys = jax.random.split(jax.random.fold_in(key, 17), 3)

    def faces(face_key):
        values = jnp.exp(jax.random.uniform(face_key, (SOLID_ALONG_NUM, SOLID_ACROSS_NUM, SPAN_NODE_COUNT), jnp.float32, jnp.log(0.2), jnp.log(2.0)))
        return values
    lower_x = faces(face_keys[0]).at[0].set(0.0)
    lower_y = faces(face_keys[1]).at[:, 0].set(0.0)
    lower_z = faces(face_keys[2])
    lower_z = jnp.where((jnp.arange(SPAN_NODE_COUNT) % UNIT_SPAN_NODES == 0)[None, None, :], 0.0, lower_z)
    upper_x = jnp.concatenate([lower_x[1:], jnp.zeros_like(lower_x[:1])], axis=0)
    upper_y = jnp.concatenate([lower_y[:, 1:], jnp.zeros_like(lower_y[:, :1])], axis=1)
    upper_z = jnp.concatenate([lower_z[:, :, 1:], jnp.zeros_like(lower_z[:, :, :1])], axis=2)
    return jnp.stack([lower_x, lower_y, lower_z, upper_x, upper_y, upper_z]).astype(jnp.float32)


def place_ends(values, own_key, low, high):
    extent = values.shape
    spot = [jax.random.randint(jax.random.fold_in(own_key, axis), (), 0, extent[axis]) for axis in range(len(extent))]
    values = values.at[tuple(spot)].set(low)
    longest = extent.index(max(extent))
    spot[longest] = (spot[longest] + 1) % extent[longest]
    return values.at[tuple(spot)].set(high)


def block_levels(stream_key, shape, pieces, least, top_value):
    def one(axis_at, shards_of):
        heights = jax.random.uniform(jax.random.fold_in(jax.random.fold_in(stream_key, 6), axis_at), (shards_of,), jnp.float32, least / len(pieces), top_value / len(pieces))
        return jnp.repeat(jnp.exp(heights), shape[axis_at] // shards_of).reshape((-1,) + (1,) * (len(shape) - axis_at - 1))

    gain = one(*pieces[0])
    for cut in pieces[1:]:
        gain = gain * one(*cut)
    return gain


def centred(stream_key, extent, deviation, most, shards=(), kind=jnp.bfloat16):
    values = jax.random.normal(stream_key, extent, jnp.float32) * deviation
    if len(shards) > 0:
        values = block_levels(stream_key, extent, shards, -0.22, 0.18) * values
    return jnp.clip(values, min=-most, max=most).astype(kind)


def setup_inputs(seed: int = 0) -> dict:
    keys = jax.random.split(jax.random.key(seed), 9)
    return {
        "mass_per_volume": jnp.clip(0.8 + 0.40000004 * jax.random.uniform(keys[0], (NX, NY, SPAN_NODE_COUNT), jnp.float32) ** block_levels(keys[0], (NX, NY, SPAN_NODE_COUNT), ((0, 8), (1, 8), (2, 12)), -0.2, 0.2), 0.8, 1.2),
        "flow_speed_vector": centred(keys[1], (3, NX, NY, SPAN_NODE_COUNT), 0.3, 1.0, ((1, 8), (2, 8), (3, 12)), jnp.float32),
        "normal_stress": jnp.clip(0.8 + 0.40000004 * jax.random.uniform(keys[2], (NX, NY, SPAN_NODE_COUNT), jnp.float32) ** block_levels(keys[2], (NX, NY, SPAN_NODE_COUNT), ((0, 8), (1, 8), (2, 12)), -0.2, 0.2), 0.8, 1.2),
        "facing_strip_index": draw_facing_strip_index(jax.random.fold_in(keys[8], 71), 0),
        "solid_kelvin": jnp.clip(0.5 + 1.0 * jax.random.uniform(keys[4], (SOLID_ALONG_NUM, SOLID_ACROSS_NUM, SPAN_NODE_COUNT), jnp.float32) ** block_levels(keys[4], (SOLID_ALONG_NUM, SOLID_ACROSS_NUM, SPAN_NODE_COUNT), ((0, 8), (1, 8), (2, 12)), -0.2, 0.2), 0.5, 1.5),
        "face_coupling": draw_face_coupling(jax.random.fold_in(keys[8], 71), 0),
        "substance_index": place_ends(jax.random.randint(keys[6], (SOLID_ALONG_NUM, SOLID_ACROSS_NUM, SPAN_NODE_COUNT), 0, MATS), jax.random.fold_in(keys[6], 1), 0, MATS - 1).astype(jnp.int32),
        "substance_storage": jnp.clip(jnp.exp(jax.random.uniform(keys[7], (MATS,), jnp.float32, math.log(0.5), math.log(4.0))), 0.5, 4.0),
    }


gamma_gas = 1.4
time_step = 0.1
viscosity = 0.05
film_coeff = 1.0
third_part = 1.0 / 3.0
two_thirds = 2.0 / 3.0

def cut_faces(values, axis_id, start_at, stop_at):
    first_space = values.ndim - 3
    indexer = [slice(None)] * values.ndim
    for member in range(3):
        if member == axis_id:
            indexer[first_space + member] = slice(start_at, stop_at)
        else:
            indexer[first_space + member] = slice(1, -1)
    return values[tuple(indexer)]

def cut_along(values, axis_id, start_at, stop_at):
    indexer = [slice(None)] * values.ndim
    indexer[values.ndim - 3 + axis_id] = slice(start_at, stop_at)
    return values[tuple(indexer)]

def crop_cells(values, margin):
    return values[..., margin:-margin, margin:-margin, margin:-margin]

def advance_rate(padded, source):
    mass_per_volume = padded[0]
    flow_speed_vector = padded[1:4] / mass_per_volume
    kinetic = 0.5 * lax.optimization_barrier(jnp.sum(padded[1:4] * flow_speed_vector, axis=0))
    normal_stress = (gamma_gas - 1.0) * (padded[4] - kinetic)
    sound_speed = jnp.sqrt(gamma_gas * normal_stress / mass_per_volume)
    interior = crop_cells(padded, 1)
    rate_sum = jnp.zeros_like(interior)
    smooth_sum = jnp.zeros_like(interior)
    for axis_id in range(3):
        along_vel = flow_speed_vector[axis_id]
        flux_dir = padded * along_vel
        flux_dir = flux_dir.at[1 + axis_id].add(normal_stress)
        flux_dir = flux_dir.at[4].add(normal_stress * along_vel)
        wave_speed = jnp.abs(along_vel) + sound_speed
        left_flux = cut_faces(flux_dir, axis_id, 0, -1)
        right_flux = cut_faces(flux_dir, axis_id, 1, None)
        left_state = cut_faces(padded, axis_id, 0, -1)
        right_state = cut_faces(padded, axis_id, 1, None)
        face_speed = jnp.maximum(cut_faces(wave_speed, axis_id, 0, -1), cut_faces(wave_speed, axis_id, 1, None))
        face_flux = 0.5 * (left_flux + right_flux) - 0.5 * face_speed * (right_state - left_state)
        rate_sum = rate_sum - (cut_along(face_flux, axis_id, 1, None) - cut_along(face_flux, axis_id, 0, -1))
        line_cut = cut_faces(padded, axis_id, None, None)
        smooth_sum = smooth_sum + (cut_along(line_cut, axis_id, 2, None) - 2.0 * cut_along(line_cut, axis_id, 1, -1) + cut_along(line_cut, axis_id, 0, -2))
    weights = jnp.array([0.0, 1.0, 1.0, 1.0, 1.0], jnp.float32).reshape(5, 1, 1, 1)
    rate_sum = rate_sum + viscosity * weights * smooth_sum
    return rate_sum.at[4].add(-source)

def fluid_state(mass_per_volume, flow_speed_vector, normal_stress):
    momentum = mass_per_volume[None] * flow_speed_vector
    energy = normal_stress / (gamma_gas - 1.0) + 0.5 * lax.optimization_barrier(jnp.sum(momentum * flow_speed_vector, axis=0))
    return jnp.concatenate([mass_per_volume[None], momentum, energy[None]], axis=0)

def metal_apply(padded, face_coupling, storage_coefficient):
    center = padded[1:-1, 1:-1, 1:-1]
    result = storage_coefficient * center
    result = result + face_coupling[0] * (center - padded[:-2, 1:-1, 1:-1]) + face_coupling[3] * (center - padded[2:, 1:-1, 1:-1])
    result = result + face_coupling[1] * (center - padded[1:-1, :-2, 1:-1]) + face_coupling[4] * (center - padded[1:-1, 2:, 1:-1])
    result = result + face_coupling[2] * (center - padded[1:-1, 1:-1, :-2]) + face_coupling[5] * (center - padded[1:-1, 1:-1, 2:])
    return result

def rate_global(conserved, source):
    padded = jnp.pad(conserved, ((0, 0), (1, 1), (1, 1), (1, 1)), mode='wrap')

    def slab_rate(slab_no):
        slab_cut = lax.dynamic_slice_in_dim(padded, slab_no * UNIT_SPAN_NODES, UNIT_SPAN_NODES + 2, axis=3)
        slab_source = lax.dynamic_slice_in_dim(source, slab_no * UNIT_SPAN_NODES, UNIT_SPAN_NODES, axis=2)
        return advance_rate(slab_cut, slab_source)
    rates = lax.map(slab_rate, jnp.arange(SPAN_NODE_COUNT // UNIT_SPAN_NODES, dtype=jnp.int32))
    return jnp.moveaxis(rates, 0, 3).reshape(5, NX, NY, SPAN_NODE_COUNT)

def invert_solid_conduction(solid_kelvin, face_coupling, storage_coefficient, kelvin_distribution):

    def apply_operator(field_in):
        return metal_apply(jnp.pad(field_in, 1), face_coupling, storage_coefficient)
    forcing_vector = storage_coefficient * solid_kelvin + kelvin_distribution
    converged_kelvin = solid_kelvin
    equation_misfit = forcing_vector - apply_operator(converged_kelvin)
    search_vector = equation_misfit
    norm_now = jnp.sum(equation_misfit * equation_misfit)
    for step_no in range(ITERS):
        image_dir = apply_operator(search_vector)
        search_factor = norm_now / jnp.sum(search_vector * image_dir)
        converged_kelvin = converged_kelvin + search_factor * search_vector
        equation_misfit = equation_misfit - search_factor * image_dir
        norm_next = jnp.sum(equation_misfit * equation_misfit)
        search_vector = equation_misfit + norm_next / norm_now * search_vector
        norm_now = norm_next
    return converged_kelvin

def pick_rows(table_rows, row_ids):
    return jnp.take(table_rows, row_ids, axis=0)

def sum_rows(flux_rows, row_ids):
    return jax.ops.segment_sum(flux_rows, row_ids, num_segments=UNITS_PER_VANE * UNIT_SOLID_ACROSS)

def bundled_iterative_method(pack):
    return invert_solid_conduction(pack[0], pack[1], pack[2], pack[3])

def reference(mass_per_volume, flow_speed_vector, normal_stress, facing_strip_index, solid_kelvin, face_coupling, substance_index, substance_storage):
    vane_sequence = SPAN_NODE_COUNT // UNIT_SPAN_NODES
    partition_sequence = NX // FX
    conserved = fluid_state(mass_per_volume, flow_speed_vector, normal_stress)
    face_temp = normal_stress.reshape(partition_sequence, FX, NY, SPAN_NODE_COUNT)[:, 0] / mass_per_volume.reshape(partition_sequence, FX, NY, SPAN_NODE_COUNT)[:, 0]
    face_temp = jnp.moveaxis(face_temp.reshape(partition_sequence * NY, vane_sequence, UNIT_SPAN_NODES), 1, 0)
    collected_surfaces = solid_kelvin.reshape(partition_sequence, UNIT_SOLID_ALONG, SOLID_ACROSS_NUM, SPAN_NODE_COUNT)[:, 0].reshape(UNITS_PER_VANE * UNIT_SOLID_ACROSS, vane_sequence, UNIT_SPAN_NODES)
    collected_surfaces = jnp.moveaxis(collected_surfaces, 1, 0)
    route_rows = facing_strip_index.reshape(vane_sequence, partition_sequence * NY)
    wall_seen = jax.vmap(pick_rows)(collected_surfaces, route_rows)
    heat_flux = film_coeff * (face_temp - wall_seen)
    arriving_energy = jax.vmap(sum_rows)(heat_flux, route_rows)
    sink = jnp.moveaxis(heat_flux, 0, 1).reshape(partition_sequence, NY, SPAN_NODE_COUNT)
    sink = jnp.zeros((partition_sequence, FX, NY, SPAN_NODE_COUNT), jnp.float32).at[:, 0].set(sink).reshape(NX, NY, SPAN_NODE_COUNT)
    present_iterate = conserved
    for section_no in range(3):
        fresh = present_iterate + time_step * rate_global(present_iterate, sink)
        if section_no == 0:
            present_iterate = fresh
        elif section_no == 1:
            present_iterate = 0.75 * conserved + 0.25 * fresh
        else:
            present_iterate = third_part * conserved + two_thirds * fresh
    storage_coefficient = substance_storage[substance_index]

    def vane_portion(values):
        return jnp.moveaxis(values.reshape(values.shape[:-1] + (vane_sequence, UNIT_SPAN_NODES)), -2, 0)
    kelvin_distribution = jnp.zeros((vane_sequence, partition_sequence, UNIT_SOLID_ALONG, SOLID_ACROSS_NUM, UNIT_SPAN_NODES), jnp.float32)
    kelvin_distribution = kelvin_distribution.at[:, :, 0].set(arriving_energy.reshape(vane_sequence, partition_sequence, SOLID_ACROSS_NUM, UNIT_SPAN_NODES)).reshape(vane_sequence, SOLID_ALONG_NUM, SOLID_ACROSS_NUM, UNIT_SPAN_NODES)
    solid_outcome = lax.map(bundled_iterative_method, (vane_portion(solid_kelvin), vane_portion(face_coupling), vane_portion(storage_coefficient), kelvin_distribution))
    metal_next = jnp.moveaxis(solid_outcome, 0, 2).reshape(SOLID_ALONG_NUM, SOLID_ACROSS_NUM, SPAN_NODE_COUNT)
    return (present_iterate, metal_next)
```

```python
import jax
import jax.numpy as jnp
from jax import lax
from jax.experimental import pallas as pl
from jax.experimental.pallas import tpu as pltpu
from jax.sharding import PartitionSpec as P

ITERS = 4
DT = 0.1
NU = 0.05
GM1 = 0.4
GAMMA = 1.4
SHIFT = 8.0
WIDTH = 8.0
ID = pl.DeviceIdType.MESH
F32 = jnp.float32


def primitives(u):
    inv = 1.0 / u[0]
    vel = [u[1] * inv, u[2] * inv, u[3] * inv]
    kin = 0.5 * (u[1] * vel[0] + u[2] * vel[1] + u[3] * vel[2])
    p = GM1 * (u[4] - kin)
    c = jnp.sqrt(GAMMA * p * inv)
    return vel[0], vel[1], vel[2], p, c


def flux(u, vel, p, d):
    out = [u[1 + d], u[1] * vel, u[2] * vel, u[3] * vel, (u[4] + p) * vel]
    out[1 + d] = out[1 + d] + p
    return out


def face(lo, hi):
    s = jnp.maximum(lo[2], hi[2])
    sv = s + 2.0 * NU
    return [
        (lo[1][f] + hi[1][f]) - (s if f == 0 else sv) * (hi[0][f] - lo[0][f])
        for f in range(5)
    ]


def kernel(
    rho_ref, vel_ref, p_ref, idx_ref, x0_ref, fc_ref, mat_ref, cap_ref,
    fluid_ref, metal_ref,
    us, pr, hz, yp, yr, zp, zr, sink, ft,
    rb1, rw, hc, rhc, wb, rwb,
    fm, pk_lo, pk_hi, rl, rh, wm, fr, qk_lo, qk_hi, ql, qh, vk, mom, rmom,
    b1_s, b1_r, y1_s, y1_r, y2_s, y2_r, b2_s, b2_r, fs, frv, ms, mr, rs, rr_, as_, ar,
):
    me_g = lax.axis_index("grp")
    me_b = lax.axis_index("blk")
    me_s = lax.axis_index("sub")
    ng = lax.axis_size("grp")
    nb = lax.axis_size("blk")
    nsub = lax.axis_size("sub")

    def blk(k):
        return lax.rem(me_b + (k + nb), nb)

    def sub(k):
        return lax.rem(me_s + (k + nsub), nsub)

    def grp(k):
        return lax.rem(me_g + (k + ng), ng)

    zlo, zhi = {"grp": grp(-1)}, {"grp": grp(1)}
    partners = [{"blk": blk(k)} for k in range(1, nb)]
    partners += [{"sub": sub(k)} for k in range(1, nsub)]
    partners += [zlo, zhi]
    partners += [{"blk": blk(i), "sub": sub(j)} for i in (-1, 1) for j in (-1, 1)]
    barrier = pltpu.get_barrier_semaphore()
    for d in partners:
        pl.semaphore_signal(barrier, inc=1, device_id=d, device_id_type=ID)

    def rcopy(src, dst, s, r, dev):
        return pltpu.make_async_remote_copy(
            src_ref=src, dst_ref=dst, send_sem=s, recv_sem=r, device_id=dev, device_id_type=ID
        )

    lane8 = lax.broadcasted_iota(jnp.int32, (8, 128), 1)
    sub8 = lax.broadcasted_iota(jnp.int32, (8, 128), 0)
    low4 = sub8 < 4

    def start_x(x, _):
        rho = rho_ref[x]
        v = [vel_ref[k, x] for k in range(3)]
        mo = [rho * a for a in v]
        us[0, 0, 1 + x, 8:40, :] = rho
        for k in range(3):
            us[0, 1 + k, 1 + x, 8:40, :] = mo[k]
        us[0, 4, 1 + x, 8:40, :] = p_ref[x] / GM1 + 0.5 * (
            mo[0] * v[0] + mo[1] * v[1] + mo[2] * v[2]
        )
        return 0

    lax.fori_loop(0, 4, start_x, 0)

    def pack_fluid(st):
        lane = lax.broadcasted_iota(jnp.int32, (32, 128), 1)
        acc = jnp.zeros((32, 128), F32)
        for x in range(4):
            for f in range(5):
                j = x * 5 + f
                yp[st, 0, j : j + 1, :] = us[st, f, 1 + x, 8:9, :]
                yp[st, 1, j : j + 1, :] = us[st, f, 1 + x, 39:40, :]
                tile = pltpu.roll(us[st, f, 1 + x, 8:40, :], 2 * j + 1, 1)
                acc = jnp.where((lane == 2 * j) | (lane == 2 * j + 1), tile, acc)
        zp[st] = acc

    def fluid_copies(st):
        rows = pl.ds(8, 32)
        return [
            rcopy(us.at[st, :, 1, rows, :], us.at[st, :, 5, rows, :], fs.at[st, 0], frv.at[st, 0], {"blk": blk(-1)}),
            rcopy(us.at[st, :, 4, rows, :], us.at[st, :, 0, rows, :], fs.at[st, 1], frv.at[st, 1], {"blk": blk(1)}),
            rcopy(yp.at[st, 0], yr.at[st, 1], fs.at[st, 2], frv.at[st, 2], {"sub": sub(-1)}),
            rcopy(yp.at[st, 1], yr.at[st, 0], fs.at[st, 3], frv.at[st, 3], {"sub": sub(1)}),
            rcopy(zp.at[st], zr.at[st, 0], fs.at[st, 4], frv.at[st, 4], zhi),
            rcopy(zp.at[st], zr.at[st, 1], fs.at[st, 5], frv.at[st, 5], zlo),
        ]

    pack_fluid(0)

    idx = idx_ref[0]
    dev_of = lax.shift_right_logical(idx, 3)
    slot1 = ((idx & 7) + 1).astype(F32)
    hot = lax.broadcasted_iota(jnp.int32, (64, 32), 0) == jnp.broadcast_to(dev_of, (64, 32))
    face_temp = p_ref[0] / rho_ref[0]
    by_dev = jnp.dot(
        hot.astype(F32), face_temp, precision=lax.Precision.HIGHEST, preferred_element_type=F32
    )
    slot_of = jnp.sum(jnp.where(hot, jnp.broadcast_to(slot1, (64, 32)), 0.0), axis=1, keepdims=True)
    slot_rows = jnp.broadcast_to(slot_of, (64, 128))
    for m in range(8):
        ft[m, 0] = by_dev[8 * m : 8 * m + 8]
        ft[m, 1] = slot_rows[8 * m : 8 * m + 8]

    for x in range(8):
        mat = mat_ref[x]
        cap = jnp.zeros((8, 128), F32)
        for m in range(8):
            cap = jnp.where(mat == m, cap_ref[m], cap)
        k = [fc_ref[f, x] for f in range(6)]
        diag = cap + ((k[0] + k[3]) + (k[1] + k[4]) + (k[2] + k[5]))
        fm[0, 4 + x] = x0_ref[x]
        fm[1, 4 + x] = (diag - SHIFT) * (1.0 / WIDTH)
        for f in range(3):
            fm[2 + f, 4 + x] = k[f] * (1.0 / WIDTH)

    def pack_metal(field, lo, hi):
        for t in range(4):
            a, b = field(2 * t), field(2 * t + 1)
            lo[t] = jnp.where(low4, a, pltpu.roll(b, 4, 0))
            hi[t] = jnp.where(low4, pltpu.roll(a, 4, 0), b)

    for f in range(5):
        pack_metal(lambda x: fm[f, 4 + x], pk_lo.at[f], pk_hi.at[f])

    def metal_copies(body, lo, hi, dl, dh, s, r):
        def cut(ref, a, b):
            return ref.at[:, a:b]

        return [
            rcopy(cut(body, 8, 12), cut(body, 0, 4), s.at[0], r.at[0], {"blk": blk(1)}),
            rcopy(cut(body, 4, 8), cut(body, 12, 16), s.at[1], r.at[1], {"blk": blk(-1)}),
            rcopy(hi, cut(dl, 2, 6), s.at[2], r.at[2], {"sub": sub(1)}),
            rcopy(lo, cut(dh, 2, 6), s.at[3], r.at[3], {"sub": sub(-1)}),
            rcopy(cut(hi, 2, 4), cut(dl, 0, 2), s.at[4], r.at[4], {"blk": blk(1), "sub": sub(1)}),
            rcopy(cut(hi, 0, 2), cut(dl, 6, 8), s.at[5], r.at[5], {"blk": blk(-1), "sub": sub(1)}),
            rcopy(cut(lo, 2, 4), cut(dh, 0, 2), s.at[6], r.at[6], {"blk": blk(1), "sub": sub(-1)}),
            rcopy(cut(lo, 0, 2), cut(dh, 6, 8), s.at[7], r.at[7], {"blk": blk(-1), "sub": sub(-1)}),
        ]

    rb1[me_b] = ft[me_b]
    rw[me_s] = x0_ref[0]

    pl.semaphore_wait(barrier, len(partners))

    for k in range(1, nb):
        to = blk(k)
        rcopy(ft.at[to], rb1.at[me_b], b1_s, b1_r, {"blk": to}).start()
    for k in range(1, nsub):
        rcopy(x0_ref.at[0], rw.at[me_s], y1_s, y1_r, {"sub": sub(k)}).start()
    halo = [fluid_copies(st) for st in range(3)]
    for c in halo[0]:
        c.start()
    coarse = metal_copies(fm, pk_lo, pk_hi, rl, rh, ms, mr)
    for c in coarse:
        c.start()

    def prims_at(st, x, r0, n):
        u = [us[st, f, x, r0 : r0 + n, :] for f in range(5)]
        for k, val in enumerate(primitives(u)):
            pr[k, x, r0 : r0 + n, :] = val

    def own_prims(st):
        def body(x, _):
            prims_at(st, x, 8, 32)
            return 0

        lax.fori_loop(1, 5, body, 0)

    def halo_in(st):
        for c in halo[st]:
            c.wait_recv()
        for x in range(4):
            for f in range(5):
                j = x * 5 + f
                us[st, f, 1 + x, 7:8, :] = yr[st, 0, j : j + 1, :]
                us[st, f, 1 + x, 40:41, :] = yr[st, 1, j : j + 1, :]
        prims_at(st, 0, 8, 32)
        prims_at(st, 5, 8, 32)
        lane = lax.broadcasted_iota(jnp.int32, (32, 128), 1)
        both = jnp.where((lane & 1) == 0, zr[st, 0], pltpu.roll(zr[st, 1], 126, 1))

        def body(x, _):
            prims_at(st, 1 + x, 0, 8)
            prims_at(st, 1 + x, 40, 8)
            u = [pltpu.roll(both, 128 - 2 * (x * 5 + f), 1) for f in range(5)]
            q = primitives(u)
            for f in range(5):
                hz[f, x] = u[f]
            for f, val in enumerate((q[2], q[3], q[4])):
                hz[5 + f, x] = val
            return 0

        lax.fori_loop(0, 4, body, 0)

    def stage(st, with_sink):
        first, last = lane8 == 0, lane8 == 127

        def body(x, _):
            for t in range(4):
                r = 8 + 8 * t

                def cells(dx, dr, d):
                    u = [us[st, f, 1 + x + dx, r + dr : r + dr + 8, :] for f in range(5)]
                    v = pr[d, 1 + x + dx, r + dr : r + dr + 8, :]
                    p = pr[3, 1 + x + dx, r + dr : r + dr + 8, :]
                    c = pr[4, 1 + x + dx, r + dr : r + dr + 8, :]
                    return u, flux(u, v, p, d), jnp.abs(v) + c

                mid = [cells(0, 0, d) for d in range(3)]
                u = mid[0][0]
                rate = None
                for d, lo, hi in (
                    (0, cells(-1, 0, 0), cells(1, 0, 0)),
                    (1, cells(0, -1, 1), cells(0, 1, 1)),
                ):
                    g0, g1 = face(lo, mid[d]), face(mid[d], hi)
                    part = [a - b for a, b in zip(g0, g1)]
                    rate = part if rate is None else [a + b for a, b in zip(rate, part)]
                h = [hz[f, x, r - 8 : r, :] for f in range(8)]
                q = list(u) + [pr[k, 1 + x, r : r + 8, :] for k in (2, 3, 4)]
                for shift, edge, low in ((1, first, True), (127, last, False)):
                    n = [jnp.where(edge, a, pltpu.roll(b, shift, 1)) for a, b in zip(h, q)]
                    other = (n[:5], flux(n[:5], n[5], n[6], 2), jnp.abs(n[5]) + n[7])
                    if low:
                        rate = [a + b for a, b in zip(rate, face(other, mid[2]))]
                    else:
                        rate = [a - b for a, b in zip(rate, face(mid[2], other))]
                for f in range(5):
                    new = u[f] + (0.5 * DT) * rate[f]
                    if with_sink and f == 4:
                        new = new - DT * sink[x, r - 8 : r, :]
                    if st == 1:
                        new = 0.75 * us[0, f, 1 + x, r : r + 8, :] + 0.25 * new
                    if st == 2:
                        new = (1.0 / 3.0) * us[0, f, 1 + x, r : r + 8, :] + (2.0 / 3.0) * new
                        fluid_ref[f, x, r - 8 : r, :] = new
                    else:
                        us[st + 1, f, 1 + x, r : r + 8, :] = new
            return 0

        lax.fori_loop(0, 4, body, 0)

    own_prims(0)

    def wait_all(buf, s, r, dev):
        d = rcopy(buf, buf, s, r, dev)
        return d

    near_b, near_s = {"blk": blk(1)}, {"sub": sub(1)}

    wait_all(rb1.at[0:7], b1_s, b1_r, near_b).wait_recv()

    def gather_strips(m, _):
        total = jnp.zeros((8, 128), F32)
        count = jnp.zeros((8, 128), F32)
        want = (sub8 + 1).astype(F32)
        for b in range(8):
            val = jnp.broadcast_to(rb1[b, 0, pl.ds(m, 1), :], (8, 128))
            slot = jnp.broadcast_to(rb1[b, 1, pl.ds(m, 1), :], (8, 128))
            here = slot == want
            total = total + jnp.where(here, val, 0.0)
            count = count + jnp.where(here, 1.0, 0.0)
        hc[m, 0] = total
        hc[m, 1] = count
        return 0

    lax.fori_loop(0, 8, gather_strips, 0)
    rhc[me_s] = hc[me_s]
    for k in range(1, nsub):
        to = sub(k)
        rcopy(hc.at[to], rhc.at[me_s], y2_s, y2_r, {"sub": to}).start()

    wait_all(rw.at[0:7], y1_s, y1_r, near_s).wait_recv()
    walls = jnp.concatenate([rw[m] for m in range(8)], axis=0)
    slots = jnp.concatenate([rb1[b, 1] for b in range(8)], axis=0)[:, 0:64]
    row = lax.broadcasted_iota(jnp.int32, (64, 64), 0)
    col = lax.broadcasted_iota(jnp.int32, (64, 64), 1)
    pick = (lax.shift_right_logical(col, 3) == (row & 7)) & (((col & 7) + 1).astype(F32) == slots)
    wall_rows = jnp.dot(
        pick.astype(F32), walls, precision=lax.Precision.HIGHEST, preferred_element_type=F32
    )
    for b in range(8):
        wb[b] = wall_rows[8 * b : 8 * b + 8]
    rwb[me_b] = wb[me_b]
    for k in range(1, nb):
        to = blk(k)
        rcopy(wb.at[to], rwb.at[me_b], b2_s, b2_r, {"blk": to}).start()

    halo_in(0)
    stage(0, False)

    wait_all(rwb.at[0:7], b2_s, b2_r, near_b).wait_recv()
    lane32 = lax.broadcasted_iota(jnp.int32, (32, 128), 1)
    sub32 = lax.broadcasted_iota(jnp.int32, (32, 32), 0)
    eye = sub32 == lax.broadcasted_iota(jnp.int32, (32, 32), 1)
    dev_f = jnp.broadcast_to(dev_of.astype(F32), (32, 32))
    dev_col = jnp.sum(jnp.where(eye, dev_f, 0.0), axis=1, keepdims=True)
    hot_t = lax.broadcasted_iota(jnp.int32, (32, 64), 1).astype(F32) == jnp.broadcast_to(dev_col, (32, 64))
    seen = jnp.concatenate([rwb[b] for b in range(8)], axis=0)
    wall_seen = jnp.dot(
        hot_t.astype(F32), seen, precision=lax.Precision.HIGHEST, preferred_element_type=F32
    )
    heat_flux = p_ref[0] / rho_ref[0] - wall_seen
    sink[0] = heat_flux
    for x in range(1, 4):
        sink[x] = jnp.zeros((32, 128), F32)
    us[1, 4, 1, 8:40, :] = us[1, 4, 1, 8:40, :] - DT * heat_flux
    pack_fluid(1)
    for c in halo[1]:
        c.start()

    for c in coarse:
        c.wait_recv()

    def window(x, mid, lo, hi, odd):
        turned = pltpu.roll(mid, 4, 0)
        if odd:
            lo = pltpu.roll(lo, 4, 0)
        else:
            hi = pltpu.roll(hi, 4, 0)
        return jnp.where(low4, lo, turned), jnp.where(low4, turned, hi)

    def build(f, _):
        for x in range(16):
            w0, w1 = window(x, fm[f, x], rl[f, x // 2], rh[f, x // 2], x % 2)
            wm[f, x, 0:8, :] = w0
            wm[f, x, 8:16, :] = w1
        return 0

    lax.fori_loop(0, 5, build, 0)

    def laplace(x):
        v = wm[0, x]
        ky, kz = wm[3, x], wm[4, x]
        gy = ky * (v - pltpu.roll(v, 1, 0))
        gz = kz * (v - pltpu.roll(v, 1, 1))
        out = wm[2, x] * (v - wm[0, x - 1]) + wm[2, x + 1] * (v - wm[0, x + 1])
        return out + (gy - pltpu.roll(gy, 15, 0)) + (gz - pltpu.roll(gz, 127, 1))

    wait_all(rhc.at[0:7], y2_s, y2_r, near_s).wait_recv()
    total = rhc[0, 0]
    count = rhc[0, 1]
    for m in range(1, 8):
        total = total + rhc[m, 0]
        count = count + rhc[m, 1]
    heat_in = total - count * x0_ref[0]

    def start_r(x, _):
        lap = laplace(4 + x)
        fr[0, 4 + x] = pltpu.roll(jnp.where(low4, lap[8:16], lap[0:8]), 4, 0) * (-WIDTH)
        return 0

    lax.fori_loop(0, 8, start_r, 0)
    fr[0, 4] = fr[0, 4] + heat_in
    pack_metal(lambda x: fr[0, 4 + x], qk_lo.at[0], qk_hi.at[0])
    fine = metal_copies(fr, qk_lo, qk_hi, ql, qh, rs, rr_)
    for c in fine:
        c.start()

    own_prims(1)
    halo_in(1)
    stage(1, True)
    pack_fluid(2)
    for c in halo[2]:
        c.start()

    for c in fine:
        c.wait_recv()
    for x in range(16):
        w0, w1 = window(x, fr[0, x], ql[0, x // 2], qh[0, x // 2], x % 2)
        vk[0, x, 0:8, :] = w0
        vk[0, x, 8:16, :] = w1

    for n in range(4):

        def apply(x, _):
            v = vk[n, x]
            ky, kz = wm[3, x], wm[4, x]
            out = wm[1, x] * v - wm[2, x] * vk[n, x - 1] - wm[2, x + 1] * vk[n, x + 1]
            out = out - ky * pltpu.roll(v, 1, 0) - pltpu.roll(ky, 15, 0) * pltpu.roll(v, 15, 0)
            out = out - kz * pltpu.roll(v, 1, 1) - pltpu.roll(kz, 127, 1) * pltpu.roll(v, 127, 1)
            vk[n + 1, x] = out
            return 0

        lax.fori_loop(n + 1, 15 - n, apply, 0)

    def dots(x, acc):
        v = [vk[n, x, 4:12, :] for n in range(5)]
        return tuple(a + v[k // 2] * v[(k + 1) // 2] for k, a in enumerate(acc))

    acc = lax.fori_loop(4, 12, dots, tuple(jnp.zeros((8, 128), F32) for _ in range(8)))
    tile = jnp.zeros((8, 128), F32)
    for k in range(8):
        tile = jnp.where(sub8 == k, jnp.sum(acc[k], axis=0, keepdims=True), tile)
    col8 = jnp.sum(tile, axis=1, keepdims=True)
    mom[...] = jnp.sum(jnp.where(lane8 == sub8, col8, 0.0), axis=0, keepdims=True)
    mine = me_b * 8 + me_s
    rmom[mine] = mom[...]

    def send_moments(k, _):
        to = {
            "blk": lax.rem(me_b + k // 8, 8),
            "sub": lax.rem(me_s + k % 8, 8),
        }
        rcopy(mom, rmom.at[mine], as_, ar, to).start()
        return 0

    lax.fori_loop(1, 64, send_moments, 0)

    own_prims(2)
    halo_in(2)
    stage(2, True)

    wait_all(rmom.at[0:63], as_, ar, near_b).wait_recv()
    sums = jnp.sum(rmom[...], axis=0)
    lane1 = lax.broadcasted_iota(jnp.int32, (1, 128), 1)
    m = [jnp.sum(jnp.where(lane1 == k, sums, 0.0), axis=1, keepdims=True) for k in range(8)]

    def product(p, q):
        out = None
        for i, a in enumerate(p):
            inner = None
            for j, b in enumerate(q):
                inner = m[i + j] * b if inner is None else inner + m[i + j] * b
            out = a * inner if out is None else out + a * inner
        return out

    def times_a(p):
        out = [SHIFT * a for a in p] + [jnp.zeros_like(p[0])]
        for i, a in enumerate(p):
            out[i + 1] = out[i + 1] + WIDTH * a
        return out

    def ratio(a, b):
        ok = b > 0.0
        return jnp.where(ok, a / jnp.where(ok, b, 1.0), 0.0)

    one = jnp.ones((1, 1), F32)
    r, d = [one], [one]
    coef = [jnp.zeros((1, 1), F32) for _ in range(4)]
    norm = m[0]
    for step in range(ITERS):
        image = times_a(d)
        alpha = ratio(norm, product(d, image))
        for i, a in enumerate(d):
            coef[i] = coef[i] + alpha * a
        if step == ITERS - 1:
            break
        r = [
            (r[i] if i < len(r) else 0.0) - alpha * image[i] for i in range(len(image))
        ]
        new = jnp.maximum(product(r, r), 0.0)
        beta = ratio(new, norm)
        d = [r[i] + (beta * d[i] if i < len(d) else 0.0) for i in range(len(r))]
        norm = new

    for x in range(8):
        out = x0_ref[x]
        for n in range(4):
            out = out + coef[n] * vk[n, 4 + x, 4:12, :]
        metal_ref[x] = out

    wait_all(rb1.at[0:7], b1_s, b1_r, near_b).wait_send()
    wait_all(rw.at[0:7], y1_s, y1_r, near_s).wait_send()
    wait_all(rhc.at[0:7], y2_s, y2_r, near_s).wait_send()
    wait_all(rwb.at[0:7], b2_s, b2_r, near_b).wait_send()
    for c in halo[0] + halo[1] + halo[2] + coarse + fine:
        c.wait_send()
    wait_all(rmom.at[0:63], as_, ar, near_b).wait_send()


def shards(rho, vel, p, idx, x0, fc, mat, cap):
    vmem = pl.BlockSpec(memory_space=pltpu.VMEM)
    dma = pltpu.SemaphoreType.DMA

    def buf(*shape):
        return pltpu.VMEM(shape, F32)

    return pl.pallas_call(
        kernel,
        out_shape=(
            jax.ShapeDtypeStruct((5, 4, 32, 128), F32),
            jax.ShapeDtypeStruct((8, 8, 128), F32),
        ),
        in_specs=[vmem] * 7 + [pl.BlockSpec(memory_space=pltpu.SMEM)],
        out_specs=(vmem, vmem),
        scratch_shapes=[
            buf(3, 5, 6, 48, 128), buf(5, 6, 48, 128), buf(8, 4, 32, 128),
            buf(3, 2, 24, 128), buf(3, 2, 24, 128), buf(3, 32, 128), buf(3, 2, 32, 128),
            buf(4, 32, 128), buf(8, 2, 8, 128),
            buf(8, 2, 8, 128), buf(8, 8, 128), buf(8, 2, 8, 128), buf(8, 2, 8, 128),
            buf(8, 8, 128), buf(8, 8, 128),
            buf(5, 16, 8, 128), buf(5, 4, 8, 128), buf(5, 4, 8, 128),
            buf(5, 8, 8, 128), buf(5, 8, 8, 128), buf(5, 16, 16, 128),
            buf(1, 16, 8, 128), buf(1, 4, 8, 128), buf(1, 4, 8, 128),
            buf(1, 8, 8, 128), buf(1, 8, 8, 128), buf(5, 16, 16, 128),
            buf(1, 128), buf(64, 1, 128),
            dma, dma, dma, dma, dma, dma, dma, dma,
            dma((3, 6)), dma((3, 6)), dma((8,)), dma((8,)), dma((8,)), dma((8,)), dma, dma,
        ],
        compiler_params=pltpu.CompilerParams(
            collective_id=0, has_side_effects=True, vmem_limit_bytes=32 * 1024 * 1024
        ),
    )(rho, vel, p, idx, x0, fc, mat, cap)


def solution(mesh):
    in_specs = (
        P("blk", "sub", "grp"),
        P(None, "blk", "sub", "grp"),
        P("blk", "sub", "grp"),
        P("grp", "blk", "sub"),
        P("blk", "sub", "grp"),
        P(None, "blk", "sub", "grp"),
        P("blk", "sub", "grp"),
        P(),
    )
    out_specs = (P(None, "blk", "sub", "grp"), P("blk", "sub", "grp"))
    return jax.shard_map(shards, mesh=mesh, in_specs=in_specs, out_specs=out_specs, check_vma=False)
```

```python
import jax
import jax.numpy as jnp
from jax import lax
from jax.experimental import pallas as pl
from jax.experimental.pallas import tpu as pltpu
from jax.sharding import PartitionSpec as P

ITERS = 4
DT = 0.1
NU = 0.05
GM1 = 0.4
GAMMA = 1.4
SHIFT = 8.0
WIDTH = 8.0
ID = pl.DeviceIdType.MESH
F32 = jnp.float32


def primitives(u):
    inv = 1.0 / u[0]
    vel = [u[1] * inv, u[2] * inv, u[3] * inv]
    kin = 0.5 * (u[1] * vel[0] + u[2] * vel[1] + u[3] * vel[2])
    p = GM1 * (u[4] - kin)
    c = jnp.sqrt(GAMMA * p * inv)
    return vel[0], vel[1], vel[2], p, c


def flux(u, vel, p, d):
    out = [u[1 + d], u[1] * vel, u[2] * vel, u[3] * vel, (u[4] + p) * vel]
    out[1 + d] = out[1 + d] + p
    return out


def face(lo, hi):
    s = jnp.maximum(lo[2], hi[2])
    sv = s + 2.0 * NU
    return [
        (lo[1][f] + hi[1][f]) - (s if f == 0 else sv) * (hi[0][f] - lo[0][f])
        for f in range(5)
    ]


def kernel(
    rho_hbm, vel_hbm, p_hbm, idx_hbm, x0_hbm, fc_hbm, mat_hbm, cap_hbm,
    fluid_ref, metal_ref,
    rho_ref, vel_ref, p_ref, idx_ref, x0_ref, fc_ref, mat_ref, cap_ref, load,
    us, pr, hz, yp, yr, zp, zr, sink, ft,
    rb1, rw, ht, hc, rhc, wb, rwb,
    fm, pk_lo, pk_hi, rl, rh, wm, wu, fr, qk_lo, qk_hi, ql, qh, vk, mom, rmom,
    b1_s, b1_r, y1_s, y1_r, y2_s, y2_r, b2_s, b2_r, fs, frv, ms, mr, rs, rr_, as_, ar,
):
    me_g = lax.axis_index("grp")
    me_b = lax.axis_index("blk")
    me_s = lax.axis_index("sub")
    ng = lax.axis_size("grp")
    nb = lax.axis_size("blk")
    nsub = lax.axis_size("sub")

    def blk(k):
        return lax.rem(me_b + (k + nb), nb)

    def sub(k):
        return lax.rem(me_s + (k + nsub), nsub)

    def grp(k):
        return lax.rem(me_g + (k + ng), ng)

    zlo, zhi = {"grp": grp(-1)}, {"grp": grp(1)}
    partners = [{"blk": blk(k)} for k in range(1, nb)]
    partners += [{"sub": sub(k)} for k in range(1, nsub)]
    partners += [zlo, zhi]
    partners += [{"blk": blk(i), "sub": sub(j)} for i in (-1, 1) for j in (-1, 1)]
    barrier = pltpu.get_barrier_semaphore()
    for d in partners:
        pl.semaphore_signal(barrier, inc=1, device_id=d, device_id_type=ID)

    pairs = (
        (idx_hbm, idx_ref), (p_hbm, p_ref), (rho_hbm, rho_ref), (x0_hbm, x0_ref), (vel_hbm, vel_ref),
        (cap_hbm, cap_ref), (mat_hbm, mat_ref), (fc_hbm, fc_ref),
    )
    loads = [pltpu.make_async_copy(a, b, load.at[n]) for n, (a, b) in enumerate(pairs)]
    for c in loads:
        c.start()

    def rcopy(src, dst, s, r, dev):
        return pltpu.make_async_remote_copy(
            src_ref=src, dst_ref=dst, send_sem=s, recv_sem=r, device_id=dev, device_id_type=ID
        )

    lane8 = lax.broadcasted_iota(jnp.int32, (8, 128), 1)
    sub8 = lax.broadcasted_iota(jnp.int32, (8, 128), 0)
    low4 = sub8 < 4

    for c in loads[0:3]:
        c.wait()

    idx = idx_ref[0]
    dev_of = lax.shift_right_logical(idx, 3)
    slot1 = ((idx & 7) + 1).astype(F32)
    hot = lax.broadcasted_iota(jnp.int32, (64, 32), 0) == jnp.broadcast_to(dev_of, (64, 32))
    face_temp = p_ref[0] / rho_ref[0]
    by_dev = jnp.dot(
        hot.astype(F32), face_temp, precision=lax.Precision.HIGHEST, preferred_element_type=F32
    )
    slot_of = jnp.sum(jnp.where(hot, jnp.broadcast_to(slot1, (64, 32)), 0.0), axis=1, keepdims=True)
    slot_rows = jnp.broadcast_to(slot_of, (64, 128))
    for m in range(8):
        ft[m, 0] = by_dev[8 * m : 8 * m + 8]
        ft[m, 1] = slot_rows[8 * m : 8 * m + 8]
    ft[8] = ft[0]

    rb1[me_b] = ft[pl.ds(me_b, 2)]
    loads[3].wait()
    rw[me_s] = x0_ref[0]
    loads[4].wait()

    def start_x(x, _):
        rho = rho_ref[x]
        v = [vel_ref[k, x] for k in range(3)]
        mo = [rho * a for a in v]
        us[0, 0, 1 + x, 8:40, :] = rho
        for k in range(3):
            us[0, 1 + k, 1 + x, 8:40, :] = mo[k]
        us[0, 4, 1 + x, 8:40, :] = p_ref[x] / GM1 + 0.5 * (
            mo[0] * v[0] + mo[1] * v[1] + mo[2] * v[2]
        )
        return 0

    for x in range(4):
        start_x(x, 0)

    def pack_fluid(st):
        lane = lax.broadcasted_iota(jnp.int32, (32, 128), 1)
        acc = jnp.zeros((32, 128), F32)
        for x in range(4):
            for f in range(5):
                j = x * 5 + f
                yp[st, 0, j : j + 1, :] = us[st, f, 1 + x, 8:9, :]
                yp[st, 1, j : j + 1, :] = us[st, f, 1 + x, 39:40, :]
                tile = pltpu.roll(us[st, f, 1 + x, 8:40, :], 2 * j + 1, 1)
                acc = jnp.where((lane == 2 * j) | (lane == 2 * j + 1), tile, acc)
        zp[st] = acc

    def fluid_copies(st):
        rows = pl.ds(8, 32)
        return [
            rcopy(us.at[st, :, 1, rows, :], us.at[st, :, 5, rows, :], fs.at[st, 0], frv.at[st, 0], {"blk": blk(-1)}),
            rcopy(us.at[st, :, 4, rows, :], us.at[st, :, 0, rows, :], fs.at[st, 1], frv.at[st, 1], {"blk": blk(1)}),
            rcopy(yp.at[st, 0], yr.at[st, 1], fs.at[st, 2], frv.at[st, 2], {"sub": sub(-1)}),
            rcopy(yp.at[st, 1], yr.at[st, 0], fs.at[st, 3], frv.at[st, 3], {"sub": sub(1)}),
            rcopy(zp.at[st], zr.at[st, 0], fs.at[st, 4], frv.at[st, 4], zhi),
            rcopy(zp.at[st], zr.at[st, 1], fs.at[st, 5], frv.at[st, 5], zlo),
        ]

    pack_fluid(0)

    for c in loads[5:8]:
        c.wait()

    for x in range(8):
        mat = mat_ref[x]
        cap = jnp.zeros((8, 128), F32)
        for m in range(8):
            cap = jnp.where(mat == m, cap_ref[m], cap)
        k = [fc_ref[f, x] for f in range(6)]
        diag = cap + ((k[0] + k[3]) + (k[1] + k[4]) + (k[2] + k[5]))
        fm[0, 4 + x] = x0_ref[x]
        fm[1, 4 + x] = (diag - SHIFT) * (1.0 / WIDTH)
        for f in range(3):
            fm[2 + f, 4 + x] = k[f] * (1.0 / WIDTH)

    def pack_metal(field, lo, hi):
        for t in range(4):
            a, b = field(2 * t), field(2 * t + 1)
            lo[t] = jnp.where(low4, a, pltpu.roll(b, 4, 0))
            hi[t] = jnp.where(low4, pltpu.roll(a, 4, 0), b)

    for f in range(5):
        pack_metal(lambda x: fm[f, 4 + x], pk_lo.at[f], pk_hi.at[f])

    def metal_copies(body, lo, hi, dl, dh, s, r):
        def cut(ref, a, b):
            return ref.at[:, a:b]

        return [
            rcopy(cut(body, 8, 12), cut(body, 0, 4), s.at[0], r.at[0], {"blk": blk(1)}),
            rcopy(cut(body, 4, 8), cut(body, 12, 16), s.at[1], r.at[1], {"blk": blk(-1)}),
            rcopy(hi, cut(dl, 2, 6), s.at[2], r.at[2], {"sub": sub(1)}),
            rcopy(lo, cut(dh, 2, 6), s.at[3], r.at[3], {"sub": sub(-1)}),
            rcopy(cut(hi, 2, 4), cut(dl, 0, 2), s.at[4], r.at[4], {"blk": blk(1), "sub": sub(1)}),
            rcopy(cut(hi, 0, 2), cut(dl, 6, 8), s.at[5], r.at[5], {"blk": blk(-1), "sub": sub(1)}),
            rcopy(cut(lo, 2, 4), cut(dh, 0, 2), s.at[6], r.at[6], {"blk": blk(1), "sub": sub(-1)}),
            rcopy(cut(lo, 0, 2), cut(dh, 6, 8), s.at[7], r.at[7], {"blk": blk(-1), "sub": sub(-1)}),
        ]

    pl.semaphore_wait(barrier, len(partners))

    for k in range(1, nb):
        to = blk(k)
        rcopy(ft.at[pl.ds(to, 2)], rb1.at[me_b], b1_s, b1_r, {"blk": to}).start()
    for k in range(1, nsub):
        rcopy(x0_ref.at[0], rw.at[me_s], y1_s, y1_r, {"sub": sub(k)}).start()
    halo = [fluid_copies(st) for st in range(3)]
    for c in halo[0]:
        c.start()
    coarse = metal_copies(fm, pk_lo, pk_hi, rl, rh, ms, mr)
    for c in coarse:
        c.start()

    def prims_at(st, x, r0, n):
        u = [us[st, f, x, r0 : r0 + n, :] for f in range(5)]
        for k, val in enumerate(primitives(u)):
            pr[k, x, r0 : r0 + n, :] = val

    def own_prims(st):
        for x in range(1, 5):
            prims_at(st, x, 8, 32)

    def halo_in(st):
        for c in halo[st]:
            c.wait_recv()
        for x in range(4):
            for f in range(5):
                j = x * 5 + f
                us[st, f, 1 + x, 7:8, :] = yr[st, 0, j : j + 1, :]
                us[st, f, 1 + x, 40:41, :] = yr[st, 1, j : j + 1, :]
        prims_at(st, 0, 8, 32)
        prims_at(st, 5, 8, 32)
        lane = lax.broadcasted_iota(jnp.int32, (32, 128), 1)
        both = jnp.where((lane & 1) == 0, zr[st, 0], pltpu.roll(zr[st, 1], 126, 1))

        for x in range(4):
            prims_at(st, 1 + x, 0, 8)
            prims_at(st, 1 + x, 40, 8)
            u = [pltpu.roll(both, (128 - 2 * (x * 5 + f)) % 128, 1) for f in range(5)]
            q = primitives(u)
            for f in range(5):
                hz[f, x] = u[f]
            for f, val in enumerate((q[2], q[3], q[4])):
                hz[5 + f, x] = val

    def stage(st, with_sink):
        first, last = lane8 == 0, lane8 == 127

        def body(x, _):
            for t in range(4):
                r = 8 + 8 * t

                def cells(dx, dr, d):
                    u = [us[st, f, 1 + x + dx, r + dr : r + dr + 8, :] for f in range(5)]
                    v = pr[d, 1 + x + dx, r + dr : r + dr + 8, :]
                    p = pr[3, 1 + x + dx, r + dr : r + dr + 8, :]
                    c = pr[4, 1 + x + dx, r + dr : r + dr + 8, :]
                    return u, flux(u, v, p, d), jnp.abs(v) + c

                mid = [cells(0, 0, d) for d in range(3)]
                u = mid[0][0]
                rate = None
                for d, lo, hi in (
                    (0, cells(-1, 0, 0), cells(1, 0, 0)),
                    (1, cells(0, -1, 1), cells(0, 1, 1)),
                ):
                    g0, g1 = face(lo, mid[d]), face(mid[d], hi)
                    part = [a - b for a, b in zip(g0, g1)]
                    rate = part if rate is None else [a + b for a, b in zip(rate, part)]
                h = [hz[f, x, r - 8 : r, :] for f in range(8)]
                q = list(u) + [pr[k, 1 + x, r : r + 8, :] for k in (2, 3, 4)]
                for shift, edge, low in ((1, first, True), (127, last, False)):
                    n = [jnp.where(edge, a, pltpu.roll(b, shift, 1)) for a, b in zip(h, q)]
                    other = (n[:5], flux(n[:5], n[5], n[6], 2), jnp.abs(n[5]) + n[7])
                    if low:
                        rate = [a + b for a, b in zip(rate, face(other, mid[2]))]
                    else:
                        rate = [a - b for a, b in zip(rate, face(mid[2], other))]
                for f in range(5):
                    new = u[f] + (0.5 * DT) * rate[f]
                    if with_sink and f == 4:
                        new = new - DT * sink[x, r - 8 : r, :]
                    if st == 1:
                        new = 0.75 * us[0, f, 1 + x, r : r + 8, :] + 0.25 * new
                    if st == 2:
                        new = (1.0 / 3.0) * us[0, f, 1 + x, r : r + 8, :] + (2.0 / 3.0) * new
                        fluid_ref[f, x, r - 8 : r, :] = new
                    else:
                        us[st + 1, f, 1 + x, r : r + 8, :] = new
            return 0

        lax.fori_loop(0, 4, body, 0)

    own_prims(0)

    def wait_all(buf, s, r, dev):
        d = rcopy(buf, buf, s, r, dev)
        return d

    near_b, near_s = {"blk": blk(1)}, {"sub": sub(1)}

    wait_all(rb1.at[0:7], b1_s, b1_r, near_b).wait_recv()

    want = (sub8 + 1).astype(F32)

    def gather_strips(m, _):
        for o in range(2):
            total = jnp.zeros((8, 128), F32)
            count = jnp.zeros((8, 128), F32)
            for b in range(8):
                val = jnp.broadcast_to(rb1[b, o, 0, pl.ds(m, 1), :], (8, 128))
                slot = jnp.broadcast_to(rb1[b, o, 1, pl.ds(m, 1), :], (8, 128))
                here = slot == want
                total = total + jnp.where(here, val, 0.0)
                count = count + jnp.where(here, 1.0, 0.0)
            ht[m, o, 0] = pltpu.roll(total, 4, 0)
            ht[m, o, 1] = pltpu.roll(count, 4, 0)
        return 0

    lax.fori_loop(0, 8, gather_strips, 0)
    for m in range(8):
        counts = jnp.zeros((8, 128), F32)
        for o in range(2):
            for t, (a, b) in enumerate((((m + 7) % 8, m), (m, (m + 1) % 8))):
                hc[m, 2 * o + t] = jnp.where(low4, ht[a, o, 0], ht[b, o, 0])
                counts = jnp.where(
                    lane8 == 2 * o + t, jnp.where(low4, ht[a, o, 1], ht[b, o, 1]), counts
                )
        hc[m, 4] = counts
    rhc[me_s] = hc[me_s]
    for k in range(1, nsub):
        to = sub(k)
        rcopy(hc.at[to], rhc.at[me_s], y2_s, y2_r, {"sub": to}).start()

    wait_all(rw.at[0:7], y1_s, y1_r, near_s).wait_recv()
    walls = jnp.concatenate([rw[m] for m in range(8)], axis=0)
    slots = jnp.concatenate([rb1[b, 0, 1] for b in range(8)], axis=0)[:, 0:64]
    row = lax.broadcasted_iota(jnp.int32, (64, 64), 0)
    col = lax.broadcasted_iota(jnp.int32, (64, 64), 1)
    pick = (lax.shift_right_logical(col, 3) == (row & 7)) & (((col & 7) + 1).astype(F32) == slots)
    wall_rows = jnp.dot(
        pick.astype(F32), walls, precision=lax.Precision.HIGHEST, preferred_element_type=F32
    )
    for b in range(8):
        wb[b] = wall_rows[8 * b : 8 * b + 8]
    rwb[me_b] = wb[me_b]
    for k in range(1, nb):
        to = blk(k)
        rcopy(wb.at[to], rwb.at[me_b], b2_s, b2_r, {"blk": to}).start()

    for c in coarse:
        c.wait_recv()

    def window(x, mid, lo, hi, odd):
        turned = pltpu.roll(mid, 4, 0)
        if odd:
            lo = pltpu.roll(lo, 4, 0)
        else:
            hi = pltpu.roll(hi, 4, 0)
        return jnp.where(low4, lo, turned), jnp.where(low4, turned, hi)

    def build(f, _):
        for x in range(16):
            w0, w1 = window(x, fm[f, x], rl[f, x // 2], rh[f, x // 2], x % 2)
            wm[f, x, 0:8, :] = w0
            wm[f, x, 8:16, :] = w1
        return 0

    lax.fori_loop(0, 5, build, 0)
    for x in range(1, 15):
        wu[0, x] = pltpu.roll(wm[3, x], 15, 0)
        wu[1, x] = pltpu.roll(wm[4, x], 127, 1)

    def laplace(x):
        v = wm[0, x]
        ky, kz = wm[3, x], wm[4, x]
        gy = ky * (v - pltpu.roll(v, 1, 0))
        gz = kz * (v - pltpu.roll(v, 1, 1))
        out = wm[2, x] * (v - wm[0, x - 1]) + wm[2, x + 1] * (v - wm[0, x + 1])
        return out + (gy - pltpu.roll(gy, 15, 0)) + (gz - pltpu.roll(gz, 127, 1))

    for x in range(8):
        lap = laplace(4 + x)
        fr[0, 4 + x] = pltpu.roll(jnp.where(low4, lap[8:16], lap[0:8]), 4, 0) * (-WIDTH)
    pack_metal(lambda x: fr[0, 4 + x], qk_lo.at[0], qk_hi.at[0])
    fine = metal_copies(fr, qk_lo, qk_hi, ql, qh, rs, rr_)
    for c in fine:
        c.start()

    halo_in(0)
    stage(0, False)

    wait_all(rwb.at[0:7], b2_s, b2_r, near_b).wait_recv()
    lane32 = lax.broadcasted_iota(jnp.int32, (32, 128), 1)
    sub32 = lax.broadcasted_iota(jnp.int32, (32, 32), 0)
    eye = sub32 == lax.broadcasted_iota(jnp.int32, (32, 32), 1)
    dev_f = jnp.broadcast_to(dev_of.astype(F32), (32, 32))
    dev_col = jnp.sum(jnp.where(eye, dev_f, 0.0), axis=1, keepdims=True)
    hot_t = lax.broadcasted_iota(jnp.int32, (32, 64), 1).astype(F32) == jnp.broadcast_to(dev_col, (32, 64))
    seen = jnp.concatenate([rwb[b] for b in range(8)], axis=0)
    wall_seen = jnp.dot(
        hot_t.astype(F32), seen, precision=lax.Precision.HIGHEST, preferred_element_type=F32
    )
    heat_flux = p_ref[0] / rho_ref[0] - wall_seen
    sink[0] = heat_flux
    for x in range(1, 4):
        sink[x] = jnp.zeros((32, 128), F32)
    us[1, 4, 1, 8:40, :] = us[1, 4, 1, 8:40, :] - DT * heat_flux
    pack_fluid(1)
    for c in halo[1]:
        c.start()
    own_prims(1)

    for c in fine:
        c.wait_recv()
    for x in range(16):
        w0, w1 = window(x, fr[0, x], ql[0, x // 2], qh[0, x // 2], x % 2)
        vk[0, x, 0:8, :] = w0
        vk[0, x, 8:16, :] = w1
    wait_all(rhc.at[0:7], y2_s, y2_r, near_s).wait_recv()
    arrived = []
    for t in range(5):
        total = rhc[0, t]
        for m in range(1, 8):
            total = total + rhc[m, t]
        arrived.append(total)
    for o, x in ((0, 4), (1, 12)):
        for t in range(2):
            count = jnp.sum(jnp.where(lane8 == 2 * o + t, arrived[4], 0.0), axis=1, keepdims=True)
            rows = slice(8 * t, 8 * t + 8)
            vk[0, x, rows, :] = vk[0, x, rows, :] + (arrived[2 * o + t] - count * wm[0, x, rows, :])

    for n in range(4):

        for x in range(n + 1, 15 - n):
            v = vk[n, x]
            out = wm[1, x] * v - wm[2, x] * vk[n, x - 1] - wm[2, x + 1] * vk[n, x + 1]
            out = out - wm[3, x] * pltpu.roll(v, 1, 0) - wu[0, x] * pltpu.roll(v, 15, 0)
            out = out - wm[4, x] * pltpu.roll(v, 1, 1) - wu[1, x] * pltpu.roll(v, 127, 1)
            vk[n + 1, x] = out

    acc = [jnp.zeros((8, 128), F32) for _ in range(8)]
    for x in range(4, 12):
        v = [vk[n, x, 4:12, :] for n in range(5)]
        acc = [a + v[k // 2] * v[(k + 1) // 2] for k, a in enumerate(acc)]
    tile = jnp.zeros((8, 128), F32)
    for k in range(8):
        tile = jnp.where(sub8 == k, jnp.sum(acc[k], axis=0, keepdims=True), tile)
    col8 = jnp.sum(tile, axis=1, keepdims=True)
    mom[...] = jnp.sum(jnp.where(lane8 == sub8, col8, 0.0), axis=0, keepdims=True)
    mine = me_b * 8 + me_s
    rmom[mine] = mom[...]

    def send_moments(k, _):
        to = {
            "blk": lax.rem(me_b + k // 8, 8),
            "sub": lax.rem(me_s + k % 8, 8),
        }
        rcopy(mom, rmom.at[mine], as_, ar, to).start()
        return 0

    lax.fori_loop(1, 64, send_moments, 0)

    halo_in(1)
    stage(1, True)
    pack_fluid(2)
    for c in halo[2]:
        c.start()

    own_prims(2)
    halo_in(2)
    stage(2, True)

    wait_all(rmom.at[0:63], as_, ar, near_b).wait_recv()
    sums = jnp.sum(rmom[...], axis=0)
    lane1 = lax.broadcasted_iota(jnp.int32, (1, 128), 1)
    m = [jnp.sum(jnp.where(lane1 == k, sums, 0.0), axis=1, keepdims=True) for k in range(8)]

    def product(p, q):
        out = None
        for i, a in enumerate(p):
            inner = None
            for j, b in enumerate(q):
                inner = m[i + j] * b if inner is None else inner + m[i + j] * b
            out = a * inner if out is None else out + a * inner
        return out

    def times_a(p):
        out = [SHIFT * a for a in p] + [jnp.zeros_like(p[0])]
        for i, a in enumerate(p):
            out[i + 1] = out[i + 1] + WIDTH * a
        return out

    def ratio(a, b):
        ok = b > 0.0
        return jnp.where(ok, a / jnp.where(ok, b, 1.0), 0.0)

    one = jnp.ones((1, 1), F32)
    r, d = [one], [one]
    coef = [jnp.zeros((1, 1), F32) for _ in range(4)]
    norm = m[0]
    for step in range(ITERS):
        image = times_a(d)
        alpha = ratio(norm, product(d, image))
        for i, a in enumerate(d):
            coef[i] = coef[i] + alpha * a
        if step == ITERS - 1:
            break
        r = [
            (r[i] if i < len(r) else 0.0) - alpha * image[i] for i in range(len(image))
        ]
        new = jnp.maximum(product(r, r), 0.0)
        beta = ratio(new, norm)
        d = [r[i] + (beta * d[i] if i < len(d) else 0.0) for i in range(len(r))]
        norm = new

    for x in range(8):
        out = x0_ref[x]
        for n in range(4):
            out = out + coef[n] * vk[n, 4 + x, 4:12, :]
        metal_ref[x] = out

    wait_all(rb1.at[0:7], b1_s, b1_r, near_b).wait_send()
    wait_all(rw.at[0:7], y1_s, y1_r, near_s).wait_send()
    wait_all(rhc.at[0:7], y2_s, y2_r, near_s).wait_send()
    wait_all(rwb.at[0:7], b2_s, b2_r, near_b).wait_send()
    for c in halo[0] + halo[1] + halo[2] + coarse + fine:
        c.wait_send()
    wait_all(rmom.at[0:63], as_, ar, near_b).wait_send()


def shards(rho, vel, p, idx, x0, fc, mat, cap):
    vmem = pl.BlockSpec(memory_space=pltpu.VMEM)
    dma = pltpu.SemaphoreType.DMA

    def buf(*shape):
        return pltpu.VMEM(shape, F32)

    return pl.pallas_call(
        kernel,
        out_shape=(
            jax.ShapeDtypeStruct((5, 4, 32, 128), F32),
            jax.ShapeDtypeStruct((8, 8, 128), F32),
        ),
        in_specs=[pl.BlockSpec(memory_space=pltpu.HBM)] * 8,
        out_specs=(vmem, vmem),
        scratch_shapes=[
            buf(4, 32, 128), buf(3, 4, 32, 128), buf(4, 32, 128), pltpu.VMEM((1, 1, 32), jnp.int32),
            buf(8, 8, 128), buf(6, 8, 8, 128), pltpu.VMEM((8, 8, 128), jnp.int32), pltpu.SMEM((8,), F32), dma((8,)),
            buf(3, 5, 6, 48, 128), buf(5, 6, 48, 128), buf(8, 4, 32, 128),
            buf(3, 2, 24, 128), buf(3, 2, 24, 128), buf(3, 32, 128), buf(3, 2, 32, 128),
            buf(4, 32, 128), buf(9, 2, 8, 128),
            buf(8, 2, 2, 8, 128), buf(8, 8, 128), buf(8, 2, 2, 8, 128), buf(8, 5, 8, 128), buf(8, 5, 8, 128),
            buf(8, 8, 128), buf(8, 8, 128),
            buf(5, 16, 8, 128), buf(5, 4, 8, 128), buf(5, 4, 8, 128),
            buf(5, 8, 8, 128), buf(5, 8, 8, 128), buf(5, 16, 16, 128), buf(2, 16, 16, 128),
            buf(1, 16, 8, 128), buf(1, 4, 8, 128), buf(1, 4, 8, 128),
            buf(1, 8, 8, 128), buf(1, 8, 8, 128), buf(5, 16, 16, 128),
            buf(1, 128), buf(64, 1, 128),
            dma, dma, dma, dma, dma, dma, dma, dma,
            dma((3, 6)), dma((3, 6)), dma((8,)), dma((8,)), dma((8,)), dma((8,)), dma, dma,
        ],
        compiler_params=pltpu.CompilerParams(
            collective_id=0, has_side_effects=True, vmem_limit_bytes=56 * 1024 * 1024
        ),
    )(rho, vel, p, idx, x0, fc, mat, cap)


def solution(mesh):
    in_specs = (
        P("blk", "sub", "grp"),
        P(None, "blk", "sub", "grp"),
        P("blk", "sub", "grp"),
        P("grp", "blk", "sub"),
        P("blk", "sub", "grp"),
        P(None, "blk", "sub", "grp"),
        P("blk", "sub", "grp"),
        P(),
    )
    out_specs = (P(None, "blk", "sub", "grp"), P("blk", "sub", "grp"))
    return jax.shard_map(shards, mesh=mesh, in_specs=in_specs, out_specs=out_specs, check_vma=False)
```

```python
import jax
import jax.numpy as jnp
from jax import lax
from jax.experimental import pallas as pl
from jax.experimental.pallas import tpu as pltpu
from jax.sharding import PartitionSpec as P

ITERS = 4
DT = 0.1
NU = 0.05
GM1 = 0.4
GAMMA = 1.4
SHIFT = 8.0
WIDTH = 8.0
ID = pl.DeviceIdType.MESH
F32 = jnp.float32


def primitives(u):
    inv = 1.0 / u[0]
    vel = [u[1] * inv, u[2] * inv, u[3] * inv]
    kin = 0.5 * (u[1] * vel[0] + u[2] * vel[1] + u[3] * vel[2])
    p = GM1 * (u[4] - kin)
    c = jnp.sqrt(GAMMA * p * inv)
    return vel[0], vel[1], vel[2], p, c


def flux(u, vel, p, d):
    out = [u[1 + d], u[1] * vel, u[2] * vel, u[3] * vel, (u[4] + p) * vel]
    out[1 + d] = out[1 + d] + p
    return out


def face(lo, hi):
    s = jnp.maximum(lo[2], hi[2])
    sv = s + 2.0 * NU
    return [
        (lo[1][f] + hi[1][f]) - (s if f == 0 else sv) * (hi[0][f] - lo[0][f])
        for f in range(5)
    ]


def kernel(
    rho_hbm, vel_hbm, p_hbm, idx_hbm, x0_hbm, fc_hbm, mat_hbm, cap_hbm,
    fluid_hbm, metal_hbm,
    rho_ref, vel_ref, p_ref, idx_ref, x0_ref, fc_ref, mat_ref, cap_ref, load,
    fluid_ref, metal_ref, store,
    us, pr, hz, yp, yr, zp, zr, sink, ft,
    rb1, rw, ht, hc, rhc, wb, rwb,
    fm, pk_lo, pk_hi, rl, rh, wm, wu, fr, qk_lo, qk_hi, ql, qh, vk, mom, rmom,
    b1_s, b1_r, y1_s, y1_r, y2_s, y2_r, b2_s, b2_r, fs, frv, ms, mr, rs, rr_, as_, ar,
):
    me_g = lax.axis_index("grp")
    me_b = lax.axis_index("blk")
    me_s = lax.axis_index("sub")
    ng = lax.axis_size("grp")
    nb = lax.axis_size("blk")
    nsub = lax.axis_size("sub")

    def blk(k):
        return lax.rem(me_b + (k + nb), nb)

    def sub(k):
        return lax.rem(me_s + (k + nsub), nsub)

    def grp(k):
        return lax.rem(me_g + (k + ng), ng)

    zlo, zhi = {"grp": grp(-1)}, {"grp": grp(1)}
    far_s = (4, 3, 5, 2, 6, 1, 7)
    far_b = (4, 5, 3, 2, 6, 7, 1)
    partners = [{"blk": blk(k)} for k in far_b]
    partners += [{"sub": sub(k)} for k in far_s]
    partners += [zlo, zhi]
    partners += [{"blk": blk(i), "sub": sub(j)} for i in (-1, 1) for j in (-1, 1)]
    barrier = pltpu.get_barrier_semaphore()
    for d in partners:
        pl.semaphore_signal(barrier, inc=1, device_id=d, device_id_type=ID)

    pairs = (
        (idx_hbm, idx_ref), (p_hbm, p_ref), (rho_hbm, rho_ref), (x0_hbm, x0_ref), (vel_hbm, vel_ref),
        (cap_hbm, cap_ref), (mat_hbm, mat_ref), (fc_hbm, fc_ref),
    )
    loads = [pltpu.make_async_copy(a, b, load.at[n]) for n, (a, b) in enumerate(pairs)]
    for c in loads:
        c.start()

    def rcopy(src, dst, s, r, dev):
        return pltpu.make_async_remote_copy(
            src_ref=src, dst_ref=dst, send_sem=s, recv_sem=r, device_id=dev, device_id_type=ID
        )

    lane8 = lax.broadcasted_iota(jnp.int32, (8, 128), 1)
    sub8 = lax.broadcasted_iota(jnp.int32, (8, 128), 0)
    low4 = sub8 < 4

    for c in loads[0:3]:
        c.wait()

    idx = idx_ref[0]
    dev_of = lax.shift_right_logical(idx, 3)
    slot1 = ((idx & 7) + 1).astype(F32)
    hot = lax.broadcasted_iota(jnp.int32, (64, 32), 0) == jnp.broadcast_to(dev_of, (64, 32))
    face_temp = p_ref[0] / rho_ref[0]
    by_dev = jnp.dot(
        hot.astype(F32), face_temp, precision=lax.Precision.HIGHEST, preferred_element_type=F32
    )
    slot_of = jnp.sum(jnp.where(hot, jnp.broadcast_to(slot1, (64, 32)), 0.0), axis=1, keepdims=True)
    slot_rows = jnp.broadcast_to(slot_of, (64, 128))
    for m in range(8):
        ft[m, 0] = by_dev[8 * m : 8 * m + 8]
        ft[m, 1] = slot_rows[8 * m : 8 * m + 8]
    ft[8] = ft[0]

    rb1[me_b] = ft[pl.ds(me_b, 2)]
    loads[3].wait()
    rw[me_s] = x0_ref[0]

    pl.semaphore_wait(barrier, len(partners))
    for k in far_s:
        rcopy(x0_ref.at[0], rw.at[me_s], y1_s, y1_r, {"sub": sub(k)}).start()
    for k in far_b:
        to = blk(k)
        rcopy(ft.at[pl.ds(to, 2)], rb1.at[me_b], b1_s, b1_r, {"blk": to}).start()
    loads[4].wait()

    def start_x(x, _):
        rho = rho_ref[x]
        v = [vel_ref[k, x] for k in range(3)]
        mo = [rho * a for a in v]
        us[0, 0, 1 + x, 8:40, :] = rho
        for k in range(3):
            us[0, 1 + k, 1 + x, 8:40, :] = mo[k]
        us[0, 4, 1 + x, 8:40, :] = p_ref[x] / GM1 + 0.5 * (
            mo[0] * v[0] + mo[1] * v[1] + mo[2] * v[2]
        )
        return 0

    for x in range(4):
        start_x(x, 0)

    def pack_fluid(st):
        lane = lax.broadcasted_iota(jnp.int32, (32, 128), 1)
        acc = jnp.zeros((32, 128), F32)
        for x in range(4):
            for f in range(5):
                j = x * 5 + f
                yp[st, 0, j : j + 1, :] = us[st, f, 1 + x, 8:9, :]
                yp[st, 1, j : j + 1, :] = us[st, f, 1 + x, 39:40, :]
                tile = pltpu.roll(us[st, f, 1 + x, 8:40, :], 2 * j + 1, 1)
                acc = jnp.where((lane == 2 * j) | (lane == 2 * j + 1), tile, acc)
        zp[st] = acc

    def fluid_copies(st):
        rows = pl.ds(8, 32)
        return [
            rcopy(us.at[st, :, 4, rows, :], us.at[st, :, 0, rows, :], fs.at[st, 1], frv.at[st, 1], {"blk": blk(1)}),
            rcopy(us.at[st, 0:4, 1, rows, :], us.at[st, 0:4, 5, rows, :], fs.at[st, 0], frv.at[st, 0], {"blk": blk(-1)}),
            rcopy(us.at[st, 4, 1, rows, :], us.at[st, 4, 5, rows, :], fs.at[st, 6], frv.at[st, 6], {"blk": blk(-1)}),
            rcopy(yp.at[st, 0], yr.at[st, 1], fs.at[st, 2], frv.at[st, 2], {"sub": sub(-1)}),
            rcopy(yp.at[st, 1], yr.at[st, 0], fs.at[st, 3], frv.at[st, 3], {"sub": sub(1)}),
            rcopy(zp.at[st], zr.at[st, 0], fs.at[st, 4], frv.at[st, 4], zhi),
            rcopy(zp.at[st], zr.at[st, 1], fs.at[st, 5], frv.at[st, 5], zlo),
        ]

    pack_fluid(0)
    halo = [fluid_copies(st) for st in range(3)]
    for c in halo[0]:
        c.start()

    for c in loads[5:8]:
        c.wait()

    for x in range(8):
        mat = mat_ref[x]
        cap = jnp.zeros((8, 128), F32)
        for m in range(8):
            cap = jnp.where(mat == m, cap_ref[m], cap)
        k = [fc_ref[f, x] for f in range(6)]
        diag = cap + ((k[0] + k[3]) + (k[1] + k[4]) + (k[2] + k[5]))
        fm[0, 4 + x] = x0_ref[x]
        fm[1, 4 + x] = (diag - SHIFT) * (1.0 / WIDTH)
        for f in range(3):
            fm[2 + f, 4 + x] = k[f] * (1.0 / WIDTH)

    def pack_metal(field, lo, hi):
        for t in range(4):
            a, b = field(2 * t), field(2 * t + 1)
            lo[t] = jnp.where(low4, a, pltpu.roll(b, 4, 0))
            hi[t] = jnp.where(low4, pltpu.roll(a, 4, 0), b)

    for f in range(5):
        pack_metal(lambda x: fm[f, 4 + x], pk_lo.at[f], pk_hi.at[f])

    def metal_copies(body, lo, hi, dl, dh, s, r):
        def cut(ref, a, b):
            return ref.at[:, a:b]

        return [
            rcopy(cut(body, 8, 12), cut(body, 0, 4), s.at[0], r.at[0], {"blk": blk(1)}),
            rcopy(cut(body, 4, 8), cut(body, 12, 16), s.at[1], r.at[1], {"blk": blk(-1)}),
            rcopy(hi, cut(dl, 2, 6), s.at[2], r.at[2], {"sub": sub(1)}),
            rcopy(lo, cut(dh, 2, 6), s.at[3], r.at[3], {"sub": sub(-1)}),
            rcopy(cut(hi, 2, 4), cut(dl, 0, 2), s.at[4], r.at[4], {"blk": blk(1), "sub": sub(1)}),
            rcopy(cut(hi, 0, 2), cut(dl, 6, 8), s.at[5], r.at[5], {"blk": blk(-1), "sub": sub(1)}),
            rcopy(cut(lo, 2, 4), cut(dh, 0, 2), s.at[6], r.at[6], {"blk": blk(1), "sub": sub(-1)}),
            rcopy(cut(lo, 0, 2), cut(dh, 6, 8), s.at[7], r.at[7], {"blk": blk(-1), "sub": sub(-1)}),
        ]

    coarse = metal_copies(fm, pk_lo, pk_hi, rl, rh, ms, mr)
    for c in coarse:
        c.start()

    stores = [
        pltpu.make_async_copy(fluid_ref.at[:, x], fluid_hbm.at[:, x], store.at[x]) for x in range(4)
    ]
    stores.append(pltpu.make_async_copy(metal_ref, metal_hbm, store.at[4]))

    def prims_at(st, x, r0, n):
        u = [us[st, f, x, r0 : r0 + n, :] for f in range(5)]
        for k, val in enumerate(primitives(u)):
            pr[k, x, r0 : r0 + n, :] = val

    def own_prims(st):
        for x in range(1, 5):
            prims_at(st, x, 8, 32)

    def halo_in(st):
        for c in halo[st]:
            c.wait_recv()
        for x in range(4):
            for f in range(5):
                j = x * 5 + f
                us[st, f, 1 + x, 7:8, :] = yr[st, 0, j : j + 1, :]
                us[st, f, 1 + x, 40:41, :] = yr[st, 1, j : j + 1, :]
        prims_at(st, 0, 8, 32)
        prims_at(st, 5, 8, 32)
        lane = lax.broadcasted_iota(jnp.int32, (32, 128), 1)
        both = jnp.where((lane & 1) == 0, zr[st, 0], pltpu.roll(zr[st, 1], 126, 1))

        for x in range(4):
            prims_at(st, 1 + x, 0, 8)
            prims_at(st, 1 + x, 40, 8)
            u = [pltpu.roll(both, (128 - 2 * (x * 5 + f)) % 128, 1) for f in range(5)]
            q = primitives(u)
            for f in range(5):
                hz[f, x] = u[f]
            for f, val in enumerate((q[2], q[3], q[4])):
                hz[5 + f, x] = val

    def stage(st, with_sink):
        first, last = lane8 == 0, lane8 == 127

        def body(x):
            for t in range(4):
                r = 8 + 8 * t

                def cells(dx, dr, d):
                    u = [us[st, f, 1 + x + dx, r + dr : r + dr + 8, :] for f in range(5)]
                    v = pr[d, 1 + x + dx, r + dr : r + dr + 8, :]
                    p = pr[3, 1 + x + dx, r + dr : r + dr + 8, :]
                    c = pr[4, 1 + x + dx, r + dr : r + dr + 8, :]
                    return u, flux(u, v, p, d), jnp.abs(v) + c

                mid = [cells(0, 0, d) for d in range(3)]
                u = mid[0][0]
                rate = None
                for d, lo, hi in (
                    (0, cells(-1, 0, 0), cells(1, 0, 0)),
                    (1, cells(0, -1, 1), cells(0, 1, 1)),
                ):
                    g0, g1 = face(lo, mid[d]), face(mid[d], hi)
                    part = [a - b for a, b in zip(g0, g1)]
                    rate = part if rate is None else [a + b for a, b in zip(rate, part)]
                h = [hz[f, x, r - 8 : r, :] for f in range(8)]
                q = list(u) + [pr[k, 1 + x, r : r + 8, :] for k in (2, 3, 4)]
                for shift, edge, low in ((1, first, True), (127, last, False)):
                    n = [jnp.where(edge, a, pltpu.roll(b, shift, 1)) for a, b in zip(h, q)]
                    other = (n[:5], flux(n[:5], n[5], n[6], 2), jnp.abs(n[5]) + n[7])
                    if low:
                        rate = [a + b for a, b in zip(rate, face(other, mid[2]))]
                    else:
                        rate = [a - b for a, b in zip(rate, face(mid[2], other))]
                for f in range(5):
                    new = u[f] + (0.5 * DT) * rate[f]
                    if with_sink and f == 4:
                        new = new - DT * sink[x, r - 8 : r, :]
                    if st == 1:
                        new = 0.75 * us[0, f, 1 + x, r : r + 8, :] + 0.25 * new
                    if st == 2:
                        new = (1.0 / 3.0) * us[0, f, 1 + x, r : r + 8, :] + (2.0 / 3.0) * new
                        fluid_ref[f, x, r - 8 : r, :] = new
                    else:
                        us[st + 1, f, 1 + x, r : r + 8, :] = new
            if st == 2:
                stores[x].start()

        body(3)
        if st < 2:
            halo[st + 1][0].start()
        body(0)
        if st < 2:
            halo[st + 1][1].start()
        if st == 1:
            halo[2][2].start()
        body(1)
        body(2)

    own_prims(0)

    def wait_all(buf, s, r, dev):
        d = rcopy(buf, buf, s, r, dev)
        return d

    near_b, near_s = {"blk": blk(1)}, {"sub": sub(1)}

    wait_all(rb1.at[0:7], b1_s, b1_r, near_b).wait_recv()

    want = (sub8 + 1).astype(F32)

    def gather_strips(m, _):
        for o in range(2):
            total = jnp.zeros((8, 128), F32)
            count = jnp.zeros((8, 128), F32)
            for b in range(8):
                val = jnp.broadcast_to(rb1[b, o, 0, pl.ds(m, 1), :], (8, 128))
                slot = jnp.broadcast_to(rb1[b, o, 1, pl.ds(m, 1), :], (8, 128))
                here = slot == want
                total = total + jnp.where(here, val, 0.0)
                count = count + jnp.where(here, 1.0, 0.0)
            ht[m, o, 0] = pltpu.roll(total, 4, 0)
            ht[m, o, 1] = pltpu.roll(count, 4, 0)
        return 0

    lax.fori_loop(0, 8, gather_strips, 0)
    for m in range(8):
        counts = jnp.zeros((8, 128), F32)
        for o in range(2):
            for t, (a, b) in enumerate((((m + 7) % 8, m), (m, (m + 1) % 8))):
                hc[m, 2 * o + t] = jnp.where(low4, ht[a, o, 0], ht[b, o, 0])
                counts = jnp.where(
                    lane8 == 2 * o + t, jnp.where(low4, ht[a, o, 1], ht[b, o, 1]), counts
                )
        hc[m, 4] = counts
    rhc[me_s] = hc[me_s]
    for k in far_s:
        to = sub(k)
        rcopy(hc.at[to], rhc.at[me_s], y2_s, y2_r, {"sub": to}).start()

    wait_all(rw.at[0:7], y1_s, y1_r, near_s).wait_recv()
    walls = jnp.concatenate([rw[m] for m in range(8)], axis=0)
    slots = jnp.concatenate([rb1[b, 0, 1] for b in range(8)], axis=0)[:, 0:64]
    row = lax.broadcasted_iota(jnp.int32, (64, 64), 0)
    col = lax.broadcasted_iota(jnp.int32, (64, 64), 1)
    pick = (lax.shift_right_logical(col, 3) == (row & 7)) & (((col & 7) + 1).astype(F32) == slots)
    wall_rows = jnp.dot(
        pick.astype(F32), walls, precision=lax.Precision.HIGHEST, preferred_element_type=F32
    )
    for b in range(8):
        wb[b] = wall_rows[8 * b : 8 * b + 8]
    rwb[me_b] = wb[me_b]
    for k in far_b:
        to = blk(k)
        rcopy(wb.at[to], rwb.at[me_b], b2_s, b2_r, {"blk": to}).start()

    for c in coarse:
        c.wait_recv()

    def window(x, mid, lo, hi, odd):
        turned = pltpu.roll(mid, 4, 0)
        if odd:
            lo = pltpu.roll(lo, 4, 0)
        else:
            hi = pltpu.roll(hi, 4, 0)
        return jnp.where(low4, lo, turned), jnp.where(low4, turned, hi)

    def build(f, _):
        for x in range(16):
            w0, w1 = window(x, fm[f, x], rl[f, x // 2], rh[f, x // 2], x % 2)
            wm[f, x, 0:8, :] = w0
            wm[f, x, 8:16, :] = w1
        return 0

    lax.fori_loop(0, 5, build, 0)
    for x in range(1, 15):
        wu[0, x] = pltpu.roll(wm[3, x], 15, 0)
        wu[1, x] = pltpu.roll(wm[4, x], 127, 1)

    def laplace(x):
        v = wm[0, x]
        ky, kz = wm[3, x], wm[4, x]
        gy = ky * (v - pltpu.roll(v, 1, 0))
        gz = kz * (v - pltpu.roll(v, 1, 1))
        out = wm[2, x] * (v - wm[0, x - 1]) + wm[2, x + 1] * (v - wm[0, x + 1])
        return out + (gy - pltpu.roll(gy, 15, 0)) + (gz - pltpu.roll(gz, 127, 1))

    for x in range(8):
        lap = laplace(4 + x)
        fr[0, 4 + x] = pltpu.roll(jnp.where(low4, lap[8:16], lap[0:8]), 4, 0) * (-WIDTH)
    pack_metal(lambda x: fr[0, 4 + x], qk_lo.at[0], qk_hi.at[0])
    fine = metal_copies(fr, qk_lo, qk_hi, ql, qh, rs, rr_)
    for c in fine:
        c.start()

    halo_in(0)
    stage(0, False)

    wait_all(rwb.at[0:7], b2_s, b2_r, near_b).wait_recv()
    lane32 = lax.broadcasted_iota(jnp.int32, (32, 128), 1)
    sub32 = lax.broadcasted_iota(jnp.int32, (32, 32), 0)
    eye = sub32 == lax.broadcasted_iota(jnp.int32, (32, 32), 1)
    dev_f = jnp.broadcast_to(dev_of.astype(F32), (32, 32))
    dev_col = jnp.sum(jnp.where(eye, dev_f, 0.0), axis=1, keepdims=True)
    hot_t = lax.broadcasted_iota(jnp.int32, (32, 64), 1).astype(F32) == jnp.broadcast_to(dev_col, (32, 64))
    seen = jnp.concatenate([rwb[b] for b in range(8)], axis=0)
    wall_seen = jnp.dot(
        hot_t.astype(F32), seen, precision=lax.Precision.HIGHEST, preferred_element_type=F32
    )
    heat_flux = p_ref[0] / rho_ref[0] - wall_seen
    sink[0] = heat_flux
    for x in range(1, 4):
        sink[x] = jnp.zeros((32, 128), F32)
    us[1, 4, 1, 8:40, :] = us[1, 4, 1, 8:40, :] - DT * heat_flux
    halo[1][2].start()
    pack_fluid(1)
    for c in halo[1][3:]:
        c.start()
    own_prims(1)

    for c in fine:
        c.wait_recv()
    for x in range(16):
        w0, w1 = window(x, fr[0, x], ql[0, x // 2], qh[0, x // 2], x % 2)
        vk[0, x, 0:8, :] = w0
        vk[0, x, 8:16, :] = w1
    wait_all(rhc.at[0:7], y2_s, y2_r, near_s).wait_recv()
    arrived = []
    for t in range(5):
        total = rhc[0, t]
        for m in range(1, 8):
            total = total + rhc[m, t]
        arrived.append(total)
    for o, x in ((0, 4), (1, 12)):
        for t in range(2):
            count = jnp.sum(jnp.where(lane8 == 2 * o + t, arrived[4], 0.0), axis=1, keepdims=True)
            rows = slice(8 * t, 8 * t + 8)
            vk[0, x, rows, :] = vk[0, x, rows, :] + (arrived[2 * o + t] - count * wm[0, x, rows, :])

    for n in range(4):

        for x in range(n + 1, 15 - n):
            v = vk[n, x]
            out = wm[1, x] * v - wm[2, x] * vk[n, x - 1] - wm[2, x + 1] * vk[n, x + 1]
            out = out - wm[3, x] * pltpu.roll(v, 1, 0) - wu[0, x] * pltpu.roll(v, 15, 0)
            out = out - wm[4, x] * pltpu.roll(v, 1, 1) - wu[1, x] * pltpu.roll(v, 127, 1)
            vk[n + 1, x] = out

    acc = [jnp.zeros((8, 128), F32) for _ in range(8)]
    for x in range(4, 12):
        v = [vk[n, x, 4:12, :] for n in range(5)]
        acc = [a + v[k // 2] * v[(k + 1) // 2] for k, a in enumerate(acc)]
    tile = jnp.zeros((8, 128), F32)
    for k in range(8):
        tile = jnp.where(sub8 == k, jnp.sum(acc[k], axis=0, keepdims=True), tile)
    col8 = jnp.sum(tile, axis=1, keepdims=True)
    mom[...] = jnp.sum(jnp.where(lane8 == sub8, col8, 0.0), axis=0, keepdims=True)
    mine = me_b * 8 + me_s
    rmom[mine] = mom[...]

    for k in far_s + (0,):
        for j in far_b + (0,):
            if (j, k) != (0, 0):
                rcopy(mom, rmom.at[mine], as_, ar, {"blk": blk(j), "sub": sub(k)}).start()

    halo_in(1)
    stage(1, True)
    pack_fluid(2)
    for c in halo[2][3:]:
        c.start()

    own_prims(2)
    halo_in(2)
    stage(2, True)

    wait_all(rmom.at[0:63], as_, ar, near_b).wait_recv()
    sums = jnp.sum(rmom[...], axis=0)
    lane1 = lax.broadcasted_iota(jnp.int32, (1, 128), 1)
    m = [jnp.sum(jnp.where(lane1 == k, sums, 0.0), axis=1, keepdims=True) for k in range(8)]

    def product(p, q):
        out = None
        for i, a in enumerate(p):
            inner = None
            for j, b in enumerate(q):
                inner = m[i + j] * b if inner is None else inner + m[i + j] * b
            out = a * inner if out is None else out + a * inner
        return out

    def times_a(p):
        out = [SHIFT * a for a in p] + [jnp.zeros_like(p[0])]
        for i, a in enumerate(p):
            out[i + 1] = out[i + 1] + WIDTH * a
        return out

    def ratio(a, b):
        ok = b > 0.0
        return jnp.where(ok, a / jnp.where(ok, b, 1.0), 0.0)

    one = jnp.ones((1, 1), F32)
    r, d = [one], [one]
    coef = [jnp.zeros((1, 1), F32) for _ in range(4)]
    norm = m[0]
    for step in range(ITERS):
        image = times_a(d)
        alpha = ratio(norm, product(d, image))
        for i, a in enumerate(d):
            coef[i] = coef[i] + alpha * a
        if step == ITERS - 1:
            break
        r = [
            (r[i] if i < len(r) else 0.0) - alpha * image[i] for i in range(len(image))
        ]
        new = jnp.maximum(product(r, r), 0.0)
        beta = ratio(new, norm)
        d = [r[i] + (beta * d[i] if i < len(d) else 0.0) for i in range(len(r))]
        norm = new

    for x in range(8):
        out = x0_ref[x]
        for n in range(4):
            out = out + coef[n] * vk[n, 4 + x, 4:12, :]
        metal_ref[x] = out
    stores[4].start()

    wait_all(rb1.at[0:7], b1_s, b1_r, near_b).wait_send()
    wait_all(rw.at[0:7], y1_s, y1_r, near_s).wait_send()
    wait_all(rhc.at[0:7], y2_s, y2_r, near_s).wait_send()
    wait_all(rwb.at[0:7], b2_s, b2_r, near_b).wait_send()
    for c in halo[0] + halo[1] + halo[2] + coarse + fine:
        c.wait_send()
    wait_all(rmom.at[0:63], as_, ar, near_b).wait_send()
    for c in stores:
        c.wait()


def shards(rho, vel, p, idx, x0, fc, mat, cap):
    dma = pltpu.SemaphoreType.DMA

    def buf(*shape):
        return pltpu.VMEM(shape, F32)

    return pl.pallas_call(
        kernel,
        out_shape=(
            jax.ShapeDtypeStruct((5, 4, 32, 128), F32),
            jax.ShapeDtypeStruct((8, 8, 128), F32),
        ),
        in_specs=[pl.BlockSpec(memory_space=pltpu.HBM)] * 8,
        out_specs=(pl.BlockSpec(memory_space=pltpu.HBM),) * 2,
        scratch_shapes=[
            buf(4, 32, 128), buf(3, 4, 32, 128), buf(4, 32, 128), pltpu.VMEM((1, 1, 32), jnp.int32),
            buf(8, 8, 128), buf(6, 8, 8, 128), pltpu.VMEM((8, 8, 128), jnp.int32), pltpu.SMEM((8,), F32), dma((8,)),
            buf(5, 4, 32, 128), buf(8, 8, 128), dma((5,)),
            buf(3, 5, 6, 48, 128), buf(5, 6, 48, 128), buf(8, 4, 32, 128),
            buf(3, 2, 24, 128), buf(3, 2, 24, 128), buf(3, 32, 128), buf(3, 2, 32, 128),
            buf(4, 32, 128), buf(9, 2, 8, 128),
            buf(8, 2, 2, 8, 128), buf(8, 8, 128), buf(8, 2, 2, 8, 128), buf(8, 5, 8, 128), buf(8, 5, 8, 128),
            buf(8, 8, 128), buf(8, 8, 128),
            buf(5, 16, 8, 128), buf(5, 4, 8, 128), buf(5, 4, 8, 128),
            buf(5, 8, 8, 128), buf(5, 8, 8, 128), buf(5, 16, 16, 128), buf(2, 16, 16, 128),
            buf(1, 16, 8, 128), buf(1, 4, 8, 128), buf(1, 4, 8, 128),
            buf(1, 8, 8, 128), buf(1, 8, 8, 128), buf(5, 16, 16, 128),
            buf(1, 128), buf(64, 1, 128),
            dma, dma, dma, dma, dma, dma, dma, dma,
            dma((3, 7)), dma((3, 7)), dma((8,)), dma((8,)), dma((8,)), dma((8,)), dma, dma,
        ],
        compiler_params=pltpu.CompilerParams(
            collective_id=0, has_side_effects=True, vmem_limit_bytes=56 * 1024 * 1024
        ),
    )(rho, vel, p, idx, x0, fc, mat, cap)


def solution(mesh):
    in_specs = (
        P("blk", "sub", "grp"),
        P(None, "blk", "sub", "grp"),
        P("blk", "sub", "grp"),
        P("grp", "blk", "sub"),
        P("blk", "sub", "grp"),
        P(None, "blk", "sub", "grp"),
        P("blk", "sub", "grp"),
        P(),
    )
    out_specs = (P(None, "blk", "sub", "grp"), P("blk", "sub", "grp"))
    return jax.shard_map(shards, mesh=mesh, in_specs=in_specs, out_specs=out_specs, check_vma=False)
```

```python
import jax
import jax.numpy as jnp
from jax import lax
from jax.experimental import pallas as pl
from jax.experimental.pallas import tpu as pltpu
from jax.sharding import PartitionSpec as P

ITERS = 4
DT = 0.1
NU = 0.05
GM1 = 0.4
GAMMA = 1.4
SHIFT = 8.0
WIDTH = 8.0
ID = pl.DeviceIdType.MESH
F32 = jnp.float32


def primitives(u):
    inv = 1.0 / u[0]
    vel = [u[1] * inv, u[2] * inv, u[3] * inv]
    kin = 0.5 * (u[1] * vel[0] + u[2] * vel[1] + u[3] * vel[2])
    p = GM1 * (u[4] - kin)
    c = jnp.sqrt(GAMMA * p * inv)
    return vel[0], vel[1], vel[2], p, c


def flux(u, vel, p, d):
    out = [u[1 + d], u[1] * vel, u[2] * vel, u[3] * vel, (u[4] + p) * vel]
    out[1 + d] = out[1 + d] + p
    return out


def face(lo, hi):
    s = jnp.maximum(lo[2], hi[2])
    sv = s + 2.0 * NU
    return [
        (lo[1][f] + hi[1][f]) - (s if f == 0 else sv) * (hi[0][f] - lo[0][f])
        for f in range(5)
    ]


def kernel(
    rho_hbm, vel_hbm, p_hbm, idx_hbm, x0_hbm, fc_hbm, mat_hbm, cap_hbm,
    fluid_hbm, metal_hbm,
    rho_ref, vel_ref, p_ref, idx_ref, x0_ref, fc_ref, mat_ref, cap_ref, load,
    fluid_ref, metal_ref, store,
    us, pr, hz, yp, yr, zp, zr, sink, ft,
    rb1, rw, ht, hc, rhc, wb, rwb,
    fm, pk_lo, pk_hi, rl, rh, wm, wu, fr, qk_lo, qk_hi, ql, qh, vk, mom, rmom,
    b1_s, b1_r, y1_s, y1_r, y2_s, y2_r, b2_s, b2_r, fs, frv, ms, mr, rs, rr_, as_, ar,
):
    me_g = lax.axis_index("grp")
    me_b = lax.axis_index("blk")
    me_s = lax.axis_index("sub")
    ng = lax.axis_size("grp")
    nb = lax.axis_size("blk")
    nsub = lax.axis_size("sub")

    def blk(k):
        return lax.rem(me_b + (k + nb), nb)

    def sub(k):
        return lax.rem(me_s + (k + nsub), nsub)

    def grp(k):
        return lax.rem(me_g + (k + ng), ng)

    zlo, zhi = {"grp": grp(-1)}, {"grp": grp(1)}
    far_s = (4, 3, 5, 2, 6, 1, 7)
    far_b = (4, 5, 3, 2, 6, 7, 1)
    partners = [{"blk": blk(k)} for k in far_b]
    partners += [{"sub": sub(k)} for k in far_s]
    partners += [zlo, zhi]
    partners += [{"blk": blk(i), "sub": sub(j)} for i in (-1, 1) for j in (-1, 1)]
    barrier = pltpu.get_barrier_semaphore()
    for d in partners:
        pl.semaphore_signal(barrier, inc=1, device_id=d, device_id_type=ID)

    pairs = (
        (idx_hbm, idx_ref), (p_hbm, p_ref), (rho_hbm, rho_ref), (x0_hbm, x0_ref), (vel_hbm, vel_ref),
        (cap_hbm, cap_ref), (mat_hbm, mat_ref), (fc_hbm, fc_ref),
    )
    loads = [pltpu.make_async_copy(a, b, load.at[n]) for n, (a, b) in enumerate(pairs)]
    for c in loads:
        c.start()

    def rcopy(src, dst, s, r, dev):
        return pltpu.make_async_remote_copy(
            src_ref=src, dst_ref=dst, send_sem=s, recv_sem=r, device_id=dev, device_id_type=ID
        )

    lane8 = lax.broadcasted_iota(jnp.int32, (8, 128), 1)
    sub8 = lax.broadcasted_iota(jnp.int32, (8, 128), 0)
    low4 = sub8 < 4

    for c in loads[0:3]:
        c.wait()

    idx = idx_ref[0]
    dev_of = lax.shift_right_logical(idx, 3)
    slot1 = ((idx & 7) + 1).astype(F32)
    hot = lax.broadcasted_iota(jnp.int32, (64, 32), 0) == jnp.broadcast_to(dev_of, (64, 32))
    face_temp = p_ref[0] / rho_ref[0]
    by_dev = jnp.dot(
        hot.astype(F32), face_temp, precision=lax.Precision.HIGHEST, preferred_element_type=F32
    )
    slot_of = jnp.sum(jnp.where(hot, jnp.broadcast_to(slot1, (64, 32)), 0.0), axis=1, keepdims=True)
    slot_rows = jnp.broadcast_to(slot_of, (64, 128))
    for m in range(8):
        ft[m, 0] = by_dev[8 * m : 8 * m + 8]
        ft[m, 1] = slot_rows[8 * m : 8 * m + 8]
    ft[8] = ft[0]

    rb1[me_b] = ft[pl.ds(me_b, 2)]
    loads[3].wait()
    rw[me_s] = x0_ref[0]

    pl.semaphore_wait(barrier, len(partners))
    for k in far_s:
        rcopy(x0_ref.at[0], rw.at[me_s], y1_s, y1_r, {"sub": sub(k)}).start()
    for k in far_b:
        to = blk(k)
        rcopy(ft.at[pl.ds(to, 2)], rb1.at[me_b], b1_s, b1_r, {"blk": to}).start()
    loads[4].wait()

    def start_x(x, _):
        rho = rho_ref[x]
        v = [vel_ref[k, x] for k in range(3)]
        mo = [rho * a for a in v]
        us[0, 0, 1 + x, 8:40, :] = rho
        for k in range(3):
            us[0, 1 + k, 1 + x, 8:40, :] = mo[k]
        us[0, 4, 1 + x, 8:40, :] = p_ref[x] / GM1 + 0.5 * (
            mo[0] * v[0] + mo[1] * v[1] + mo[2] * v[2]
        )
        return 0

    for x in range(4):
        start_x(x, 0)

    def pack_fluid(st, part=range(20), more=False):
        lane = lax.broadcasted_iota(jnp.int32, (32, 128), 1)
        acc = zp[st] if more else jnp.zeros((32, 128), F32)
        for x in range(4):
            for f in range(5):
                j = x * 5 + f
                if j not in part:
                    continue
                yp[st, 0, j : j + 1, :] = us[st, f, 1 + x, 8:9, :]
                yp[st, 1, j : j + 1, :] = us[st, f, 1 + x, 39:40, :]
                tile = pltpu.roll(us[st, f, 1 + x, 8:40, :], 2 * j + 1, 1)
                acc = jnp.where((lane == 2 * j) | (lane == 2 * j + 1), tile, acc)
        zp[st] = acc

    def fluid_copies(st):
        rows = pl.ds(8, 32)
        return [
            rcopy(us.at[st, :, 4, rows, :], us.at[st, :, 0, rows, :], fs.at[st, 1], frv.at[st, 1], {"blk": blk(1)}),
            rcopy(us.at[st, 0:4, 1, rows, :], us.at[st, 0:4, 5, rows, :], fs.at[st, 0], frv.at[st, 0], {"blk": blk(-1)}),
            rcopy(us.at[st, 4, 1, rows, :], us.at[st, 4, 5, rows, :], fs.at[st, 6], frv.at[st, 6], {"blk": blk(-1)}),
            rcopy(yp.at[st, 0], yr.at[st, 1], fs.at[st, 2], frv.at[st, 2], {"sub": sub(-1)}),
            rcopy(yp.at[st, 1], yr.at[st, 0], fs.at[st, 3], frv.at[st, 3], {"sub": sub(1)}),
            rcopy(zp.at[st], zr.at[st, 0], fs.at[st, 4], frv.at[st, 4], zhi),
            rcopy(zp.at[st], zr.at[st, 1], fs.at[st, 5], frv.at[st, 5], zlo),
        ]

    pack_fluid(0)
    halo = [fluid_copies(st) for st in range(3)]
    for c in halo[0]:
        c.start()

    for c in loads[5:8]:
        c.wait()

    for x in range(8):
        mat = mat_ref[x]
        cap = jnp.zeros((8, 128), F32)
        for m in range(8):
            cap = jnp.where(mat == m, cap_ref[m], cap)
        k = [fc_ref[f, x] for f in range(6)]
        diag = cap + ((k[0] + k[3]) + (k[1] + k[4]) + (k[2] + k[5]))
        fm[0, 4 + x] = x0_ref[x]
        fm[1, 4 + x] = (diag - SHIFT) * (1.0 / WIDTH)
        for f in range(3):
            fm[2 + f, 4 + x] = k[f] * (1.0 / WIDTH)

    def pack_metal(field, lo, hi):
        for t in range(4):
            a, b = field(2 * t), field(2 * t + 1)
            lo[t] = jnp.where(low4, a, pltpu.roll(b, 4, 0))
            hi[t] = jnp.where(low4, pltpu.roll(a, 4, 0), b)

    for f in range(5):
        pack_metal(lambda x: fm[f, 4 + x], pk_lo.at[f], pk_hi.at[f])

    def metal_copies(body, lo, hi, dl, dh, s, r):
        def cut(ref, a, b):
            return ref.at[:, a:b]

        return [
            rcopy(cut(body, 8, 12), cut(body, 0, 4), s.at[0], r.at[0], {"blk": blk(1)}),
            rcopy(cut(body, 4, 8), cut(body, 12, 16), s.at[1], r.at[1], {"blk": blk(-1)}),
            rcopy(hi, cut(dl, 2, 6), s.at[2], r.at[2], {"sub": sub(1)}),
            rcopy(lo, cut(dh, 2, 6), s.at[3], r.at[3], {"sub": sub(-1)}),
            rcopy(cut(hi, 2, 4), cut(dl, 0, 2), s.at[4], r.at[4], {"blk": blk(1), "sub": sub(1)}),
            rcopy(cut(hi, 0, 2), cut(dl, 6, 8), s.at[5], r.at[5], {"blk": blk(-1), "sub": sub(1)}),
            rcopy(cut(lo, 2, 4), cut(dh, 0, 2), s.at[6], r.at[6], {"blk": blk(1), "sub": sub(-1)}),
            rcopy(cut(lo, 0, 2), cut(dh, 6, 8), s.at[7], r.at[7], {"blk": blk(-1), "sub": sub(-1)}),
        ]

    coarse = metal_copies(fm, pk_lo, pk_hi, rl, rh, ms, mr)
    for c in coarse:
        c.start()

    stores = [
        pltpu.make_async_copy(fluid_ref.at[:, x], fluid_hbm.at[:, x], store.at[x]) for x in range(4)
    ]
    stores.append(pltpu.make_async_copy(metal_ref, metal_hbm, store.at[4]))

    def prims_at(st, x, r0, n):
        u = [us[st, f, x, r0 : r0 + n, :] for f in range(5)]
        for k, val in enumerate(primitives(u)):
            pr[k, x, r0 : r0 + n, :] = val

    def own_prims(st):
        for x in range(1, 5):
            prims_at(st, x, 8, 32)

    def halo_in(st):
        for c in halo[st]:
            c.wait_recv()
        for x in range(4):
            for f in range(5):
                j = x * 5 + f
                us[st, f, 1 + x, 7:8, :] = yr[st, 0, j : j + 1, :]
                us[st, f, 1 + x, 40:41, :] = yr[st, 1, j : j + 1, :]
        prims_at(st, 0, 8, 32)
        prims_at(st, 5, 8, 32)
        lane = lax.broadcasted_iota(jnp.int32, (32, 128), 1)
        both = jnp.where((lane & 1) == 0, zr[st, 0], pltpu.roll(zr[st, 1], 126, 1))

        for x in range(4):
            prims_at(st, 1 + x, 0, 8)
            prims_at(st, 1 + x, 40, 8)
            u = [pltpu.roll(both, (128 - 2 * (x * 5 + f)) % 128, 1) for f in range(5)]
            q = primitives(u)
            for f in range(5):
                hz[f, x] = u[f]
            for f, val in enumerate((q[2], q[3], q[4])):
                hz[5 + f, x] = val

    def stage(st, with_sink):
        first, last = lane8 == 0, lane8 == 127

        def body(x):
            for t in range(4):
                r = 8 + 8 * t

                def cells(dx, dr, d):
                    u = [us[st, f, 1 + x + dx, r + dr : r + dr + 8, :] for f in range(5)]
                    v = pr[d, 1 + x + dx, r + dr : r + dr + 8, :]
                    p = pr[3, 1 + x + dx, r + dr : r + dr + 8, :]
                    c = pr[4, 1 + x + dx, r + dr : r + dr + 8, :]
                    return u, flux(u, v, p, d), jnp.abs(v) + c

                mid = [cells(0, 0, d) for d in range(3)]
                u = mid[0][0]
                rate = None
                for d, lo, hi in (
                    (0, cells(-1, 0, 0), cells(1, 0, 0)),
                    (1, cells(0, -1, 1), cells(0, 1, 1)),
                ):
                    g0, g1 = face(lo, mid[d]), face(mid[d], hi)
                    part = [a - b for a, b in zip(g0, g1)]
                    rate = part if rate is None else [a + b for a, b in zip(rate, part)]
                h = [hz[f, x, r - 8 : r, :] for f in range(8)]
                q = list(u) + [pr[k, 1 + x, r : r + 8, :] for k in (2, 3, 4)]
                for shift, edge, low in ((1, first, True), (127, last, False)):
                    n = [jnp.where(edge, a, pltpu.roll(b, shift, 1)) for a, b in zip(h, q)]
                    other = (n[:5], flux(n[:5], n[5], n[6], 2), jnp.abs(n[5]) + n[7])
                    if low:
                        rate = [a + b for a, b in zip(rate, face(other, mid[2]))]
                    else:
                        rate = [a - b for a, b in zip(rate, face(mid[2], other))]
                for f in range(5):
                    new = u[f] + (0.5 * DT) * rate[f]
                    if with_sink and f == 4:
                        new = new - DT * sink[x, r - 8 : r, :]
                    if st == 1:
                        new = 0.75 * us[0, f, 1 + x, r : r + 8, :] + 0.25 * new
                    if st == 2:
                        new = (1.0 / 3.0) * us[0, f, 1 + x, r : r + 8, :] + (2.0 / 3.0) * new
                        fluid_ref[f, x, r - 8 : r, :] = new
                    else:
                        us[st + 1, f, 1 + x, r : r + 8, :] = new
            if st == 2:
                stores[x].start()

        body(3)
        if st < 2:
            halo[st + 1][0].start()
        body(0)
        if st < 2:
            halo[st + 1][1].start()
        if st == 1:
            halo[2][2].start()
        body(1)
        body(2)

    own_prims(0)

    def wait_all(buf, s, r, dev):
        d = rcopy(buf, buf, s, r, dev)
        return d

    near_b, near_s = {"blk": blk(1)}, {"sub": sub(1)}

    wait_all(rb1.at[0:7], b1_s, b1_r, near_b).wait_recv()

    want = (sub8 + 1).astype(F32)

    def gather_strips(m, _):
        for o in range(2):
            total = jnp.zeros((8, 128), F32)
            count = jnp.zeros((8, 128), F32)
            for b in range(8):
                val = jnp.broadcast_to(rb1[b, o, 0, pl.ds(m, 1), :], (8, 128))
                slot = jnp.broadcast_to(rb1[b, o, 1, pl.ds(m, 1), :], (8, 128))
                here = slot == want
                total = total + jnp.where(here, val, 0.0)
                count = count + jnp.where(here, 1.0, 0.0)
            ht[m, o, 0] = pltpu.roll(total, 4, 0)
            ht[m, o, 1] = pltpu.roll(count, 4, 0)
        return 0

    for m in range(8):
        gather_strips(m, 0)
    for m in range(8):
        counts = jnp.zeros((8, 128), F32)
        for o in range(2):
            for t, (a, b) in enumerate((((m + 7) % 8, m), (m, (m + 1) % 8))):
                hc[m, 2 * o + t] = jnp.where(low4, ht[a, o, 0], ht[b, o, 0])
                counts = jnp.where(
                    lane8 == 2 * o + t, jnp.where(low4, ht[a, o, 1], ht[b, o, 1]), counts
                )
        hc[m, 4] = counts
    rhc[me_s] = hc[me_s]
    for k in far_s:
        to = sub(k)
        rcopy(hc.at[to], rhc.at[me_s], y2_s, y2_r, {"sub": to}).start()

    slots = jnp.concatenate([rb1[b, 0, 1] for b in range(8)], axis=0)[:, 0:64]
    row = lax.broadcasted_iota(jnp.int32, (64, 64), 0)
    col = lax.broadcasted_iota(jnp.int32, (64, 64), 1)
    pick = (lax.shift_right_logical(col, 3) == (row & 7)) & (((col & 7) + 1).astype(F32) == slots)
    wait_all(rw.at[0:7], y1_s, y1_r, near_s).wait_recv()
    walls = jnp.concatenate([rw[m] for m in range(8)], axis=0)
    wall_rows = jnp.dot(
        pick.astype(F32), walls, precision=lax.Precision.HIGHEST, preferred_element_type=F32
    )
    for b in range(8):
        wb[b] = wall_rows[8 * b : 8 * b + 8]
    rwb[me_b] = wb[me_b]
    for k in far_b:
        to = blk(k)
        rcopy(wb.at[to], rwb.at[me_b], b2_s, b2_r, {"blk": to}).start()

    for c in coarse:
        c.wait_recv()

    def window(x, mid, lo, hi, odd):
        turned = pltpu.roll(mid, 4, 0)
        if odd:
            lo = pltpu.roll(lo, 4, 0)
        else:
            hi = pltpu.roll(hi, 4, 0)
        return jnp.where(low4, lo, turned), jnp.where(low4, turned, hi)

    def build(f, _):
        for x in range(16):
            w0, w1 = window(x, fm[f, x], rl[f, x // 2], rh[f, x // 2], x % 2)
            wm[f, x, 0:8, :] = w0
            wm[f, x, 8:16, :] = w1
        return 0

    lax.fori_loop(0, 5, build, 0)
    for x in range(1, 15):
        wu[0, x] = pltpu.roll(wm[3, x], 15, 0)
        wu[1, x] = pltpu.roll(wm[4, x], 127, 1)

    def laplace(x):
        v = wm[0, x]
        ky, kz = wm[3, x], wm[4, x]
        gy = ky * (v - pltpu.roll(v, 1, 0))
        gz = kz * (v - pltpu.roll(v, 1, 1))
        out = wm[2, x] * (v - wm[0, x - 1]) + wm[2, x + 1] * (v - wm[0, x + 1])
        return out + (gy - pltpu.roll(gy, 15, 0)) + (gz - pltpu.roll(gz, 127, 1))

    for x in range(8):
        lap = laplace(4 + x)
        fr[0, 4 + x] = pltpu.roll(jnp.where(low4, lap[8:16], lap[0:8]), 4, 0) * (-WIDTH)
    pack_metal(lambda x: fr[0, 4 + x], qk_lo.at[0], qk_hi.at[0])
    fine = metal_copies(fr, qk_lo, qk_hi, ql, qh, rs, rr_)
    for c in fine:
        c.start()

    halo_in(0)
    stage(0, False)

    lane32 = lax.broadcasted_iota(jnp.int32, (32, 128), 1)
    sub32 = lax.broadcasted_iota(jnp.int32, (32, 32), 0)
    eye = sub32 == lax.broadcasted_iota(jnp.int32, (32, 32), 1)
    dev_f = jnp.broadcast_to(dev_of.astype(F32), (32, 32))
    dev_col = jnp.sum(jnp.where(eye, dev_f, 0.0), axis=1, keepdims=True)
    hot_t = lax.broadcasted_iota(jnp.int32, (32, 64), 1).astype(F32) == jnp.broadcast_to(dev_col, (32, 64))
    pack_fluid(1, [j for j in range(20) if j != 4])
    for x in range(1, 4):
        sink[x] = jnp.zeros((32, 128), F32)
    wait_all(rwb.at[0:7], b2_s, b2_r, near_b).wait_recv()
    seen = jnp.concatenate([rwb[b] for b in range(8)], axis=0)
    wall_seen = jnp.dot(
        hot_t.astype(F32), seen, precision=lax.Precision.HIGHEST, preferred_element_type=F32
    )
    heat_flux = face_temp - wall_seen
    sink[0] = heat_flux
    us[1, 4, 1, 8:40, :] = us[1, 4, 1, 8:40, :] - DT * heat_flux
    halo[1][2].start()
    pack_fluid(1, (4,), True)
    for c in halo[1][3:]:
        c.start()
    own_prims(1)

    for c in fine:
        c.wait_recv()
    for x in range(16):
        w0, w1 = window(x, fr[0, x], ql[0, x // 2], qh[0, x // 2], x % 2)
        vk[0, x, 0:8, :] = w0
        vk[0, x, 8:16, :] = w1
    wait_all(rhc.at[0:7], y2_s, y2_r, near_s).wait_recv()
    arrived = []
    for t in range(5):
        total = rhc[0, t]
        for m in range(1, 8):
            total = total + rhc[m, t]
        arrived.append(total)
    for o, x in ((0, 4), (1, 12)):
        for t in range(2):
            count = jnp.sum(jnp.where(lane8 == 2 * o + t, arrived[4], 0.0), axis=1, keepdims=True)
            rows = slice(8 * t, 8 * t + 8)
            vk[0, x, rows, :] = vk[0, x, rows, :] + (arrived[2 * o + t] - count * wm[0, x, rows, :])

    for n in range(4):

        for x in range(n + 1, 15 - n):
            v = vk[n, x]
            out = wm[1, x] * v - wm[2, x] * vk[n, x - 1] - wm[2, x + 1] * vk[n, x + 1]
            out = out - wm[3, x] * pltpu.roll(v, 1, 0) - wu[0, x] * pltpu.roll(v, 15, 0)
            out = out - wm[4, x] * pltpu.roll(v, 1, 1) - wu[1, x] * pltpu.roll(v, 127, 1)
            vk[n + 1, x] = out

    acc = [jnp.zeros((8, 128), F32) for _ in range(8)]
    for x in range(4, 12):
        v = [vk[n, x, 4:12, :] for n in range(5)]
        acc = [a + v[k // 2] * v[(k + 1) // 2] for k, a in enumerate(acc)]
    tile = jnp.zeros((8, 128), F32)
    for k in range(8):
        tile = jnp.where(sub8 == k, jnp.sum(acc[k], axis=0, keepdims=True), tile)
    col8 = jnp.sum(tile, axis=1, keepdims=True)
    mom[...] = jnp.sum(jnp.where(lane8 == sub8, col8, 0.0), axis=0, keepdims=True)
    mine = me_b * 8 + me_s
    rmom[mine] = mom[...]

    for k in far_s + (0,):
        for j in far_b + (0,):
            if (j, k) != (0, 0):
                rcopy(mom, rmom.at[mine], as_, ar, {"blk": blk(j), "sub": sub(k)}).start()

    halo_in(1)
    stage(1, True)
    pack_fluid(2)
    for c in halo[2][3:]:
        c.start()

    own_prims(2)
    halo_in(2)
    stage(2, True)

    wait_all(rmom.at[0:63], as_, ar, near_b).wait_recv()
    sums = jnp.sum(rmom[...], axis=0)
    lane1 = lax.broadcasted_iota(jnp.int32, (1, 128), 1)
    m = [jnp.sum(jnp.where(lane1 == k, sums, 0.0), axis=1, keepdims=True) for k in range(8)]

    def product(p, q):
        out = None
        for i, a in enumerate(p):
            inner = None
            for j, b in enumerate(q):
                inner = m[i + j] * b if inner is None else inner + m[i + j] * b
            out = a * inner if out is None else out + a * inner
        return out

    def times_a(p):
        out = [SHIFT * a for a in p] + [jnp.zeros_like(p[0])]
        for i, a in enumerate(p):
            out[i + 1] = out[i + 1] + WIDTH * a
        return out

    def ratio(a, b):
        ok = b > 0.0
        return jnp.where(ok, a / jnp.where(ok, b, 1.0), 0.0)

    one = jnp.ones((1, 1), F32)
    r, d = [one], [one]
    coef = [jnp.zeros((1, 1), F32) for _ in range(4)]
    norm = m[0]
    for step in range(ITERS):
        image = times_a(d)
        alpha = ratio(norm, product(d, image))
        for i, a in enumerate(d):
            coef[i] = coef[i] + alpha * a
        if step == ITERS - 1:
            break
        r = [
            (r[i] if i < len(r) else 0.0) - alpha * image[i] for i in range(len(image))
        ]
        new = jnp.maximum(product(r, r), 0.0)
        beta = ratio(new, norm)
        d = [r[i] + (beta * d[i] if i < len(d) else 0.0) for i in range(len(r))]
        norm = new

    for x in range(8):
        out = x0_ref[x]
        for n in range(4):
            out = out + coef[n] * vk[n, 4 + x, 4:12, :]
        metal_ref[x] = out
    stores[4].start()

    wait_all(rb1.at[0:7], b1_s, b1_r, near_b).wait_send()
    wait_all(rw.at[0:7], y1_s, y1_r, near_s).wait_send()
    wait_all(rhc.at[0:7], y2_s, y2_r, near_s).wait_send()
    wait_all(rwb.at[0:7], b2_s, b2_r, near_b).wait_send()
    for c in halo[0] + halo[1] + halo[2] + coarse + fine:
        c.wait_send()
    wait_all(rmom.at[0:63], as_, ar, near_b).wait_send()
    for c in stores:
        c.wait()


def shards(rho, vel, p, idx, x0, fc, mat, cap):
    dma = pltpu.SemaphoreType.DMA

    def buf(*shape):
        return pltpu.VMEM(shape, F32)

    return pl.pallas_call(
        kernel,
        out_shape=(
            jax.ShapeDtypeStruct((5, 4, 32, 128), F32),
            jax.ShapeDtypeStruct((8, 8, 128), F32),
        ),
        in_specs=[pl.BlockSpec(memory_space=pltpu.HBM)] * 8,
        out_specs=(pl.BlockSpec(memory_space=pltpu.HBM),) * 2,
        scratch_shapes=[
            buf(4, 32, 128), buf(3, 4, 32, 128), buf(4, 32, 128), pltpu.VMEM((1, 1, 32), jnp.int32),
            buf(8, 8, 128), buf(6, 8, 8, 128), pltpu.VMEM((8, 8, 128), jnp.int32), pltpu.SMEM((8,), F32), dma((8,)),
            buf(5, 4, 32, 128), buf(8, 8, 128), dma((5,)),
            buf(3, 5, 6, 48, 128), buf(5, 6, 48, 128), buf(8, 4, 32, 128),
            buf(3, 2, 24, 128), buf(3, 2, 24, 128), buf(3, 32, 128), buf(3, 2, 32, 128),
            buf(4, 32, 128), buf(9, 2, 8, 128),
            buf(8, 2, 2, 8, 128), buf(8, 8, 128), buf(8, 2, 2, 8, 128), buf(8, 5, 8, 128), buf(8, 5, 8, 128),
            buf(8, 8, 128), buf(8, 8, 128),
            buf(5, 16, 8, 128), buf(5, 4, 8, 128), buf(5, 4, 8, 128),
            buf(5, 8, 8, 128), buf(5, 8, 8, 128), buf(5, 16, 16, 128), buf(2, 16, 16, 128),
            buf(1, 16, 8, 128), buf(1, 4, 8, 128), buf(1, 4, 8, 128),
            buf(1, 8, 8, 128), buf(1, 8, 8, 128), buf(5, 16, 16, 128),
            buf(1, 128), buf(64, 1, 128),
            dma, dma, dma, dma, dma, dma, dma, dma,
            dma((3, 7)), dma((3, 7)), dma((8,)), dma((8,)), dma((8,)), dma((8,)), dma, dma,
        ],
        compiler_params=pltpu.CompilerParams(
            collective_id=0, has_side_effects=True, vmem_limit_bytes=56 * 1024 * 1024
        ),
    )(rho, vel, p, idx, x0, fc, mat, cap)


def solution(mesh):
    in_specs = (
        P("blk", "sub", "grp"),
        P(None, "blk", "sub", "grp"),
        P("blk", "sub", "grp"),
        P("grp", "blk", "sub"),
        P("blk", "sub", "grp"),
        P(None, "blk", "sub", "grp"),
        P("blk", "sub", "grp"),
        P(),
    )
    out_specs = (P(None, "blk", "sub", "grp"), P("blk", "sub", "grp"))
    return jax.shard_map(shards, mesh=mesh, in_specs=in_specs, out_specs=out_specs, check_vma=False)
```
